1024 devices in a mesh: ctx: 128 (over z, y), dp: 8 (over x, core).
Axes of the slice: x: 4, y: 8, z: 16, core: 2. Of those that a mesh axis runs over, the one named last changes fastest.
Arguments:
- queries: bfloat16 [131072, 1536], P(('dp', 'ctx')), parts along dimension 0, may hold values from -8 to 8
- latents: bfloat16 [131072, 576], P(('dp', 'ctx')), parts along dimension 0, may hold values from -8 to 8
- key_up: bfloat16 [512, 1024], replicated, may hold values from -0.25 to 0.25
- value_up: bfloat16 [512, 1024], replicated, may hold values from -0.25 to 0.25
- link_mask: int32 [1024, 128], P(('dp', 'ctx')), parts along dimension 0, may hold values from 0 to 1, as said below
- out_grad: bfloat16 [131072, 1024], P(('dp', 'ctx')), parts along dimension 0, may hold values from -6 to 6
Outputs:
- attention: bfloat16 [131072, 1024], P(('dp', 'ctx')), parts along dimension 0
- grad_queries: bfloat16 [131072, 1536], P(('dp', 'ctx')), parts along dimension 0
- grad_latents: bfloat16 [131072, 576], P(('dp', 'ctx')), parts along dimension 0
The draws below stay inside these ranges and needn't reach their ends.
There are 8 independent parts, one for each index of `dp`. The reference program is written for one: setup_inputs(seed, part) draws one part's arguments, and reference() takes and returns one part's arrays. A program takes and returns all parts, laid end to end along the dimension named above; an argument that names none is the same for every part. Nothing has to cross between parts.
Inputs may be any that keep to these rules, and one draw needn't show every extreme that they name: Entries are 0 or 1. link_mask[b, b] = 1, link_mask[b, b - 1] = 1 for b >= 1; any other 1 lies at c = b - 2 ** k for some k >= 1 with c >= 0. Each row holds at most 4 ones, and the last row exactly 4.
All inputs are finite; a program needn't handle non-finite values.
Results may differ from the reference program's by a relative error of at most 0.017.
Values may be sent and summed in bfloat16 or wider, within the bound.
A program may use at most 64 MiB of HBM per device.

```python
import jax
import jax.numpy as jnp
from jax import lax

HEADS = 8
NOPE = 128
ROPE = 64
LATENT = 512
TOK_DEV = 128
LINK_MOST = 4
BLOCKS = 128
TOKENS = 16384
LOG_CTX = 7
N_CTX = 128


def draw_queries(key, part):
    key = jax.random.fold_in(key, 21)
    total = TOK_DEV * N_CTX
    base = jnp.clip(jax.random.normal(key, (total, HEADS, NOPE + ROPE), jnp.float32), -6.0, 6.0)
    return base.reshape(total, HEADS * (NOPE + ROPE)).astype(jnp.bfloat16)


def draw_latents(key, part):
    key = jax.random.fold_in(key, 22)
    total = TOK_DEV * N_CTX
    base = jnp.clip(jax.random.normal(key, (total, LATENT + ROPE), jnp.float32), -6.0, 6.0)
    return base.astype(jnp.bfloat16)


def draw_link_mask(key, part):
    key = jax.random.fold_in(key, 23)
    first, second = jax.random.split(key)
    block_count = N_CTX
    rows = jnp.arange(block_count, dtype=jnp.int32)[:, None]
    cols = jnp.arange(block_count, dtype=jnp.int32)[None, :]
    levels = jnp.arange(1, LOG_CTX, dtype=jnp.int32)
    distance = (2 ** levels).astype(jnp.int32)[None, :]
    wanted = jax.random.randint(first, (block_count, 1), 0, 3)
    wanted = jnp.where(rows == block_count - 1, 2, wanted)
    usable = distance <= rows
    priority = jax.random.randint(second, (block_count, LOG_CTX - 1), 0, 1 << 20) * 16 + levels[None, :]
    priority = jnp.where(usable, priority, -1)
    rank = jnp.sum((priority[:, None, :] > priority[:, :, None]).astype(jnp.int32), axis=2)
    chosen = usable & (rank < wanted)
    links = jnp.sum((chosen[:, :, None] & (cols[:, None, :] == rows[:, :, None] - distance[:, :, None])).astype(jnp.int32), axis=1)
    near = ((cols == rows) | (cols == rows - 1)).astype(jnp.int32)
    return jnp.minimum(near + links, 1).astype(jnp.int32)


def level_of(key, shape, cuts, smallest, largest):
    gain, own = 1.0, jax.random.fold_in(key, 6)
    for dim, blocks in cuts:
        heights = jnp.exp(jax.random.uniform(jax.random.fold_in(own, dim), (blocks,), jnp.float32, smallest / len(cuts), largest / len(cuts)))
        gain = gain * jnp.repeat(heights, shape[dim] // blocks).reshape([-1 if axis == dim else 1 for axis in range(len(shape))])
    return gain


def normal_values(stream_key, extent, deviation, most, shards=(), held_as=jnp.bfloat16):
    entries = deviation * jax.random.normal(stream_key, extent, jnp.float32)
    if shards:
        entries = entries * level_of(stream_key, extent, shards, -0.22, 0.18)
    return jnp.clip(entries, -most, most).astype(held_as)


def setup_inputs(seed: int = 0, part: int = 0) -> dict:
    key_list = jax.random.split(jax.random.key(seed), 7)
    own_keys = jax.random.split(jax.random.fold_in(key_list[6], part), 7)
    return {
        "queries": draw_queries(jax.random.fold_in(jax.random.fold_in(key_list[6], part), 71), part),
        "latents": draw_latents(jax.random.fold_in(jax.random.fold_in(key_list[6], part), 71), part),
        "key_up": normal_values(key_list[2], (LATENT, HEADS * NOPE), LATENT ** -0.5, 0.25),
        "value_up": normal_values(key_list[3], (LATENT, HEADS * NOPE), LATENT ** -0.5, 0.25),
        "link_mask": draw_link_mask(jax.random.fold_in(jax.random.fold_in(key_list[6], part), 71), part),
        "out_grad": normal_values(own_keys[5], (TOKENS, HEADS * NOPE), 1.0, 6.0, ((0, 128),)),
    }


def reference(queries, latents, key_up, value_up, link_mask, out_grad):
    total = queries.shape[0]
    block_len = TOK_DEV
    scale = (NOPE + ROPE) ** -0.5
    plain = latents[:, :LATENT]
    keys_nope = jnp.dot(plain, key_up, preferred_element_type=jnp.float32).astype(jnp.bfloat16)
    values = jnp.dot(plain, value_up, preferred_element_type=jnp.float32).astype(jnp.bfloat16)
    rope_keys = latents[:, LATENT:]
    offsets = jnp.array([0] + [2 ** level for level in range(LOG_CTX)], jnp.int32)
    position = jnp.arange(block_len, dtype=jnp.int32)
    causal = position[:, None] >= position[None, :]

    def pick(source, index):
        return lax.dynamic_slice_in_dim(source, (index * block_len).astype(jnp.int32), block_len, 0)

    def one_block(carry, qblock):
        acc_keys, acc_values, acc_rope = carry
        start = (qblock * block_len).astype(jnp.int32)
        candidate = (qblock - offsets).astype(jnp.int32)
        safe = jnp.maximum(candidate, 0).astype(jnp.int32)
        valid = (candidate >= 0) & (link_mask[qblock, safe] == 1)
        order = jnp.argsort(jnp.where(valid, 0, 1).astype(jnp.int32), stable=True)[:LINK_MOST]
        chosen = safe[order]
        live = valid[order]
        is_diag = offsets[order] == 0
        keys_sel = jax.vmap(lambda index: pick(keys_nope, index))(chosen).reshape(LINK_MOST, block_len, HEADS, NOPE)
        vals_sel = jax.vmap(lambda index: pick(values, index))(chosen).reshape(LINK_MOST, block_len, HEADS, NOPE)
        rope_sel = jax.vmap(lambda index: pick(rope_keys, index))(chosen)
        keys_full = jnp.concatenate([keys_sel.astype(jnp.float32), jnp.broadcast_to(rope_sel.astype(jnp.float32)[:, :, None, :], (LINK_MOST, block_len, HEADS, ROPE))], axis=3)
        q_block = lax.dynamic_slice_in_dim(queries, start, block_len, 0).reshape(block_len, HEADS, NOPE + ROPE).astype(jnp.float32)
        grad_block = lax.dynamic_slice_in_dim(out_grad, start, block_len, 0).reshape(block_len, HEADS, NOPE).astype(jnp.float32)
        scores = jnp.einsum("thd,jshd->hjts", q_block, keys_full) * scale
        allowed = live[None, :, None, None] & ((~is_diag)[None, :, None, None] | causal[None, None, :, :])
        scores = jnp.where(allowed, scores, -jnp.inf)
        peak = jnp.max(scores, axis=(1, 3), keepdims=True)
        expd = jnp.exp(scores - peak)
        probs = expd / jnp.sum(expd, axis=(1, 3), keepdims=True)
        probs_bf = probs.astype(jnp.bfloat16).astype(jnp.float32)
        vals_f = vals_sel.astype(jnp.float32)
        attention = jnp.einsum("hjts,jshd->thd", probs_bf, vals_f).astype(jnp.bfloat16)
        dprobs = jnp.einsum("thd,jshd->hjts", grad_block, vals_f)
        delta = jnp.sum(probs * dprobs, axis=(1, 3), keepdims=True)
        dscores = (probs * (dprobs - delta) * scale).astype(jnp.bfloat16).astype(jnp.float32)
        grad_q = jnp.einsum("hjts,jshd->thd", dscores, keys_full).astype(jnp.bfloat16)
        pair_keys = jnp.einsum("hjts,thd->jshd", dscores, q_block[:, :, :NOPE]).astype(jnp.bfloat16).astype(jnp.float32)
        pair_values = jnp.einsum("hjts,thd->jshd", probs_bf, grad_block).astype(jnp.bfloat16).astype(jnp.float32)
        pair_rope = jnp.einsum("hjts,thd->jsd", dscores, q_block[:, :, NOPE:]).astype(jnp.bfloat16).astype(jnp.float32)
        for slot in range(LINK_MOST):
            row_start = (chosen[slot] * block_len).astype(jnp.int32)
            keep = live[slot].astype(jnp.float32)
            old_keys = lax.dynamic_slice_in_dim(acc_keys, row_start, block_len, 0)
            acc_keys = lax.dynamic_update_slice_in_dim(acc_keys, old_keys + keep * pair_keys[slot].reshape(block_len, HEADS * NOPE), row_start, 0)
            old_values = lax.dynamic_slice_in_dim(acc_values, row_start, block_len, 0)
            acc_values = lax.dynamic_update_slice_in_dim(acc_values, old_values + keep * pair_values[slot].reshape(block_len, HEADS * NOPE), row_start, 0)
            old_rope = lax.dynamic_slice_in_dim(acc_rope, row_start, block_len, 0)
            acc_rope = lax.dynamic_update_slice_in_dim(acc_rope, old_rope + keep * pair_rope[slot], row_start, 0)
        return (acc_keys, acc_values, acc_rope), (attention.reshape(block_len, HEADS * NOPE), grad_q.reshape(block_len, HEADS * (NOPE + ROPE)))

    start_carry = (jnp.zeros((total, HEADS * NOPE), jnp.float32), jnp.zeros((total, HEADS * NOPE), jnp.float32), jnp.zeros((total, ROPE), jnp.float32))
    carry, stacked = lax.scan(one_block, start_carry, jnp.arange(BLOCKS, dtype=jnp.int32))
    acc_keys, acc_values, acc_rope = carry
    attention = stacked[0].reshape(total, HEADS * NOPE)
    grad_queries = stacked[1].reshape(total, HEADS * (NOPE + ROPE))
    grad_plain = jnp.dot(acc_keys, key_up.astype(jnp.float32).T, precision=lax.Precision.HIGHEST) + jnp.dot(acc_values, value_up.astype(jnp.float32).T, precision=lax.Precision.HIGHEST)
    grad_latents = jnp.concatenate([grad_plain, acc_rope], axis=1).astype(jnp.bfloat16)
    return (attention, grad_queries, grad_latents)
```

```python
import jax
import jax.numpy as jnp
from jax import lax
from jax.experimental import pallas as pl
from jax.experimental.pallas import tpu as pltpu
from jax.sharding import PartitionSpec as P

HEADS = 8
NOPE = 128
ROPE = 64
LATENT = 512
SLOTS = 4
TOK = 128
NY = 8
NZ = 16
LEVELS = 8
WIRE = 576
PART_A = (384, 192)
PART_B = ((0, 192), (192, 192))
PARTS = (PART_A,) + PART_B
MESH = pl.DeviceIdType.MESH
F32 = jnp.float32
BF16 = jnp.bfloat16


class Move:
    def __init__(self, src, dst, dz, dy, valid):
        self.src, self.dst, self.dz, self.dy, self.valid = src, dst, dz, dy, valid


class Exchange:
    def __init__(self, moves, send_sem, recv_sem):
        self.moves, self.send_sem, self.recv_sem = moves, send_sem, recv_sem
        self.order = {name: i for i, name in enumerate(moves)}
        position = lax.axis_index("ctx")
        self.z = lax.div(position, NY)
        self.y = lax.rem(position, NY)

    def at(self, dz, dy):
        return lax.rem(self.z + dz + NZ, NZ), lax.rem(self.y + dy + NY, NY)

    def index(self, dz, dy):
        z, y = self.at(dz, dy)
        return z * NY + y

    def sends(self, name):
        return self.moves[name].valid(self.z, self.y)

    def receives(self, name):
        move = self.moves[name]
        return move.valid(*self.at(-move.dz, -move.dy))

    def barrier(self):
        barrier = pltpu.get_barrier_semaphore()
        groups = {}
        for name, move in self.moves.items():
            groups.setdefault((move.dz, move.dy), []).append(name)
        waits = jnp.int32(0)
        for (dz, dy), names in groups.items():
            out, into = self.sends(names[0]), self.receives(names[0])
            for name in names[1:]:
                out, into = out | self.sends(name), into | self.receives(name)
            waits = waits + out.astype(jnp.int32)

            @pl.when(into)
            def _():
                pl.semaphore_signal(
                    barrier, inc=1, device_id={"ctx": self.index(-dz, -dy)}, device_id_type=MESH
                )

        pl.semaphore_wait(barrier, waits)

    def copy(self, name):
        move, i = self.moves[name], self.order[name]
        return pltpu.make_async_remote_copy(
            src_ref=move.src,
            dst_ref=move.dst,
            send_sem=self.send_sem.at[i],
            recv_sem=self.recv_sem.at[i],
            device_id={"ctx": self.index(move.dz, move.dy)},
            device_id_type=MESH,
        )

    def start(self, name):
        @pl.when(self.sends(name))
        def _():
            self.copy(name).start()

    def wait(self, name):
        @pl.when(self.receives(name))
        def _():
            self.copy(name).wait_recv()

    def finish(self):
        for name in self.moves:

            @pl.when(self.sends(name))
            def _():
                self.copy(name).wait_send()


def rows(ref, part, lead=None):
    window = pl.ds(part[0], part[1])
    return ref.at[window] if lead is None else ref.at[lead, window]


def outward_moves(cand, passed):
    moves = {}
    for i, part in enumerate(PARTS):
        own, l4, l5 = rows(cand, part, 0), rows(cand, part, 4), rows(cand, part, 5)
        l6, l7 = rows(cand, part, 6), rows(cand, part, 7)
        moves["one", i] = Move(own, l4, 1, 0, lambda z, y: z < 15)
        moves["two", i] = Move(l4, l5, 1, 0, lambda z, y: (z >= 1) & (z < 15))
        moves["four", i] = Move(l5, l6, 2, 0, lambda z, y: (z >= 2) & (z < 14))
        if i == 0:
            moves["eight", i] = Move(l6, l7, 4, 0, lambda z, y: (z >= 4) & (z < 12))
        else:
            via = passed.at[i - 1]
            moves["back", i] = Move(own, via, -4, 0, lambda z, y: z < 8)
            moves["on", i] = Move(via, l7, -4, 0, lambda z, y: (z < 4) | (z >= 12))
    for k in range(3):
        by = 2**k
        moves["near", k] = Move(cand.at[0], cand.at[k + 1], 0, by, lambda z, y, by=by: y + by < NY)
        moves["cross", k] = Move(
            cand.at[4], cand.at[k + 1], 0, by, lambda z, y, by=by: (y + by >= NY) & (z >= 1)
        )
    return moves


def pack_rope(rope):
    return jnp.concatenate([rope[:64], rope[64:]], axis=1)


def gather_kernel(lat_ref, cand, passed, send_sem, recv_sem):
    for c in range(4):
        cand[0, c * 128 : (c + 1) * 128, :] = lat_ref[:, c * 128 : (c + 1) * 128]
    cand[0, 512:576, :] = pack_rope(lat_ref[:, 512:576].astype(F32)).astype(BF16)
    ex = Exchange(outward_moves(cand, passed), send_sem, recv_sem)
    ex.barrier()
    for i in (1, 2):
        ex.start(("back", i))
    for i in range(3):
        ex.start(("one", i))
    for k in (2, 1, 0):
        ex.start(("near", k))
    for i in range(3):
        ex.wait(("one", i))
        ex.start(("two", i))
    for k in (2, 1, 0):
        ex.start(("cross", k))
    for i in (1, 2):
        ex.wait(("back", i))
        ex.start(("on", i))
    for i in range(3):
        ex.wait(("two", i))
        ex.start(("four", i))
    for i in range(3):
        ex.wait(("four", i))
        if i == 0:
            ex.start(("eight", 0))
    for k in range(3):
        ex.wait(("near", k))
        ex.wait(("cross", k))
    ex.wait(("eight", 0))
    for i in (1, 2):
        ex.wait(("on", i))
    ex.finish()


def gather(latents):
    vmem = pl.BlockSpec(memory_space=pltpu.VMEM)
    count = 3 * 3 + 1 + 4 + 6
    return pl.pallas_call(
        gather_kernel,
        out_shape=jax.ShapeDtypeStruct((LEVELS, WIRE, 128), BF16),
        in_specs=[vmem],
        out_specs=vmem,
        scratch_shapes=[
            pltpu.VMEM((2, 192, 128), BF16),
            pltpu.SemaphoreType.DMA((count,)),
            pltpu.SemaphoreType.DMA((count,)),
        ],
        compiler_params=pltpu.CompilerParams(
            collective_id=0, has_side_effects=True, vmem_limit_bytes=16 * 2**20
        ),
        name="latents_out",
    )(latents)


def attend_kernel(
    mask_ref, q_ref, cand, ku_ref, vu_ref, og_ref, att_ref, gq_ref, pieces, own_ref,
    qa, keys, values, rope, pk, pv, share,
):
    position = lax.axis_index("ctx")
    rank = jnp.int32(1)
    level_of = [jnp.int32(0) for _ in range(SLOTS)]
    slot_of = [jnp.int32(0)]
    for level in range(1, LEVELS):
        source = position - 2 ** (level - 1)
        linked = (source >= 0) & (mask_ref[0, jnp.maximum(source, 0)] == 1) & (rank < SLOTS)
        for j in range(1, SLOTS):
            level_of[j] = jnp.where(linked & (rank == j), level, level_of[j])
        slot_of.append(jnp.where(linked, rank, SLOTS))
        rank = rank + linked.astype(jnp.int32)

    scale = (NOPE + ROPE) ** -0.5
    lane = lax.broadcasted_iota(jnp.int32, (64, 128), 1)
    zeros = jnp.zeros((TOK, 64), BF16)
    for h in range(HEADS):
        base = h * (NOPE + ROPE)
        qa[:, h * 256 : (h + 1) * 256] = jnp.concatenate(
            [q_ref[:, base : base + 192].astype(F32), zeros.astype(F32)], axis=1
        ).astype(BF16)
    for j in range(SLOTS):
        block = cand[level_of[j]]
        plain = jnp.concatenate([block[c * 128 : (c + 1) * 128] for c in range(4)], axis=1)
        keys[j * TOK : (j + 1) * TOK, :] = jnp.dot(
            plain, ku_ref[...], preferred_element_type=F32
        ).astype(BF16)
        values[j * TOK : (j + 1) * TOK, :] = jnp.dot(
            plain, vu_ref[...], preferred_element_type=F32
        ).astype(BF16)
        packed = block[512:576].astype(F32)
        rope[j * TOK : j * TOK + 64, :] = jnp.where(lane < 64, packed, 0.0).astype(BF16)
        rope[j * TOK + 64 : (j + 1) * TOK, :] = jnp.where(
            lane < 64, pltpu.roll(packed, 64, 1), 0.0
        ).astype(BF16)
    t = lax.broadcasted_iota(jnp.int32, (TOK, SLOTS * TOK), 0)
    s = lax.broadcasted_iota(jnp.int32, (TOK, SLOTS * TOK), 1)
    edge = jnp.where(
        s < TOK, t, jnp.where(s < rank * TOK, SLOTS * TOK, -1)
    )
    allowed = edge >= s
    nt = (((1,), (1,)), ((), ()))
    tn = (((0,), (0,)), ((), ()))
    rope_sum = jnp.zeros((SLOTS * TOK, 128), F32)
    for h in range(HEADS):
        cols = slice(h * 128, (h + 1) * 128)
        q_h = qa[:, h * 256 : (h + 1) * 256]
        k_h = jnp.concatenate([keys[:, cols], rope[...]], axis=1)
        v_h = values[:, cols]
        g_h = og_ref[:, cols]
        scores = lax.dot_general(q_h, k_h, nt, preferred_element_type=F32)
        scores = jnp.where(allowed, scores, -jnp.inf)
        peak = jnp.max(scores, axis=1, keepdims=True)
        powers = jnp.exp((scores - peak) * scale)
        probs = powers * (1.0 / jnp.sum(powers, axis=1, keepdims=True))
        probs_bf = probs.astype(BF16)
        att_ref[:, cols] = jnp.dot(probs_bf, v_h, preferred_element_type=F32).astype(BF16)
        dprobs = lax.dot_general(g_h, v_h, nt, preferred_element_type=F32)
        delta = jnp.sum(probs * dprobs, axis=1, keepdims=True)
        dscores = (probs * (dprobs - delta) * scale).astype(BF16)
        dq = jnp.dot(dscores, k_h, preferred_element_type=F32)
        base = h * (NOPE + ROPE)
        gq_ref[:, base : base + 192] = dq[:, :192].astype(BF16)
        dk = lax.dot_general(dscores, q_h, tn, preferred_element_type=F32)
        pk[:, cols] = dk[:, :128].astype(BF16)
        rope_sum = rope_sum + dk[:, 128:]
        pv[:, cols] = lax.dot_general(
            probs_bf, g_h, tn, preferred_element_type=F32
        ).astype(BF16)
    share[SLOTS] = jnp.zeros((WIRE, 128), BF16)
    for j in range(SLOTS):
        part = slice(j * TOK, (j + 1) * TOK)
        grad = lax.dot_general(pk[part], ku_ref[...], nt, preferred_element_type=F32)
        grad = grad + lax.dot_general(pv[part], vu_ref[...], nt, preferred_element_type=F32)
        turned = rope_sum[j * TOK : j * TOK + 64] + pltpu.roll(
            rope_sum[j * TOK + 64 : (j + 1) * TOK], 64, 1
        )
        for c in range(4):
            block = grad[:, c * 128 : (c + 1) * 128]
            if j == 0:
                own_ref[c * 128 : (c + 1) * 128, :] = block
            else:
                share[j, c * 128 : (c + 1) * 128, :] = block.astype(BF16)
        if j == 0:
            own_ref[512:576, :] = turned
        else:
            share[j, 512:576, :] = turned.astype(BF16)
    for level in range(1, LEVELS):
        pieces[level - 1] = share[slot_of[level]]


def attend(link_mask, queries, cand, key_up, value_up, out_grad):
    vmem = pl.BlockSpec(memory_space=pltpu.VMEM)
    width = HEADS * NOPE
    return pl.pallas_call(
        attend_kernel,
        out_shape=(
            jax.ShapeDtypeStruct((TOK, width), BF16),
            jax.ShapeDtypeStruct((TOK, HEADS * (NOPE + ROPE)), BF16),
            jax.ShapeDtypeStruct((LEVELS - 1, WIRE, 128), BF16),
            jax.ShapeDtypeStruct((WIRE, 128), F32),
        ),
        in_specs=[pl.BlockSpec(memory_space=pltpu.SMEM)] + [vmem] * 5,
        out_specs=(vmem,) * 4,
        scratch_shapes=[
            pltpu.VMEM((TOK, HEADS * 256), BF16),
            pltpu.VMEM((SLOTS * TOK, width), BF16),
            pltpu.VMEM((SLOTS * TOK, width), BF16),
            pltpu.VMEM((SLOTS * TOK, 128), BF16),
            pltpu.VMEM((SLOTS * TOK, width), BF16),
            pltpu.VMEM((SLOTS * TOK, width), BF16),
            pltpu.VMEM((SLOTS + 1, WIRE, 128), BF16),
        ],
        compiler_params=pltpu.CompilerParams(vmem_limit_bytes=48 * 2**20),
        name="attend",
    )(link_mask, queries, cand, key_up, value_up, out_grad)


def homeward_moves(pieces, r8, r4, r2, r1, t4, t2, t1, passed, far, near):
    moves = {}
    for i, part in enumerate(PARTS):
        p7 = rows(pieces, part, 6)
        if i == 0:
            moves["eight", i] = Move(p7, r8, -4, 0, lambda z, y: z >= 8)
            src = rows(t4, part)
        else:
            via, last = passed.at[i - 1], rows(far, part)
            moves["back", i] = Move(p7, via, 4, 0, lambda z, y: z >= 8)
            moves["on", i] = Move(via, last, 4, 0, lambda z, y: (z < 4) | (z >= 12))
            src = rows(pieces, part, 5)
        moves["four", i] = Move(src, rows(r4, part), -2, 0, lambda z, y: z >= 4)
        moves["two", i] = Move(rows(t2, part), rows(r2, part), -1, 0, lambda z, y: z >= 2)
        moves["one", i] = Move(rows(t1, part), rows(r1, part), -1, 0, lambda z, y: z >= 1)
    for k in range(3):
        by = 2**k
        moves["near", k] = Move(
            pieces.at[k], near.at[k], 0, -by, lambda z, y, by=by: (y >= by) | (z >= 1)
        )
    return moves


def home_kernel(
    pieces, own_ref, out_ref, r8, r4, r2, r1, t4, t2, t1, passed, far, near, send_sem, recv_sem
):
    ex = Exchange(
        homeward_moves(pieces, r8, r4, r2, r1, t4, t2, t1, passed, far, near), send_sem, recv_sem
    )
    z, y = ex.z, ex.y

    def piece(level, part):
        return pieces[level - 1, part[0] : part[0] + part[1], :].astype(F32)

    def got(ref, part, valid):
        return jnp.where(valid, ref[part[0] : part[0] + part[1], :].astype(F32), 0.0)

    ex.barrier()
    for i in (1, 2):
        ex.start(("back", i))
    ex.start(("eight", 0))
    for i in (1, 2):
        ex.start(("four", i))
    for k in (2, 1, 0):
        ex.start(("near", k))
    ex.wait(("eight", 0))
    a0, a1 = PART_A[0], PART_A[0] + PART_A[1]
    t4[a0:a1, :] = (piece(6, PART_A) + jnp.where(z <= 11, r8[...].astype(F32), 0.0)).astype(BF16)
    ex.start(("four", 0))
    for i in (1, 2):
        ex.wait(("back", i))
        ex.start(("on", i))
    for i in (1, 2, 0):
        part = PARTS[i]
        ex.wait(("four", i))
        t2[part[0] : part[0] + part[1], :] = (
            piece(5, part) + got(r4, part, z <= 13)
        ).astype(BF16)
        ex.start(("two", i))
    for k in range(3):
        ex.wait(("near", k))
    for i in (1, 2, 0):
        part = PARTS[i]
        ex.wait(("two", i))
        total = piece(4, part) + got(r2, part, z <= 14)
        for k in range(3):
            total = total + got(near.at[k], part, y + 2**k >= NY)
        t1[part[0] : part[0] + part[1], :] = total.astype(BF16)
        ex.start(("one", i))
    for i in (1, 2):
        ex.wait(("on", i))
    sums = {}
    for i in (1, 2, 0):
        part = PARTS[i]
        ex.wait(("one", i))
        total = own_ref[part[0] : part[0] + part[1], :] + got(r1, part, z <= 14)
        for k in range(3):
            total = total + got(near.at[k], part, y + 2**k < NY)
        if i > 0:
            total = total + got(far, part, z < 8)
        sums[i] = total
    whole = jnp.concatenate([sums[1], sums[2], sums[0]], axis=0)
    for c in range(4):
        out_ref[:, c * 128 : (c + 1) * 128] = whole[c * 128 : (c + 1) * 128].astype(BF16)
    turned = whole[512:576]
    out_ref[:64, 512:576] = turned[:, :64].astype(BF16)
    out_ref[64:, 512:576] = pltpu.roll(turned, 64, 1)[:, :64].astype(BF16)
    ex.finish()


def home(pieces, own):
    vmem = pl.BlockSpec(memory_space=pltpu.VMEM)
    block = pltpu.VMEM((WIRE, 128), BF16)
    count = 1 + 4 + 9 + 3
    return pl.pallas_call(
        home_kernel,
        out_shape=jax.ShapeDtypeStruct((TOK, LATENT + ROPE), BF16),
        in_specs=[vmem, vmem],
        out_specs=vmem,
        scratch_shapes=[
            pltpu.VMEM((192, 128), BF16),
            block, block, block, block, block, block,
            pltpu.VMEM((2, 192, 128), BF16),
            block,
            pltpu.VMEM((3, WIRE, 128), BF16),
            pltpu.SemaphoreType.DMA((count,)),
            pltpu.SemaphoreType.DMA((count,)),
        ],
        compiler_params=pltpu.CompilerParams(
            collective_id=1, has_side_effects=True, vmem_limit_bytes=16 * 2**20
        ),
        name="gradients_home",
    )(pieces, own)


def on_device(queries, latents, key_up, value_up, link_mask, out_grad):
    cand = gather(latents)
    attention, grad_queries, pieces, own = attend(
        link_mask, queries, cand, key_up, value_up, out_grad
    )
    return attention, grad_queries, home(pieces, own)


def solution(mesh):
    split = P(("dp", "ctx"), None)
    return jax.shard_map(
        on_device,
        mesh=mesh,
        in_specs=(split, split, P(), P(), split, split),
        out_specs=(split, split, split),
        check_vma=False,
    )
```

```python
import jax
import jax.numpy as jnp
from jax import lax
from jax.experimental import pallas as pl
from jax.experimental.pallas import tpu as pltpu
from jax.sharding import PartitionSpec as P

HEADS = 8
NOPE = 128
ROPE = 64
LATENT = 512
SLOTS = 4
TOK = 128
NY = 8
NZ = 16
LEVELS = 8
WIDTH = HEADS * NOPE
WIRE = LATENT + ROPE
PART_A = (384, 192)
PART_B = ((0, 192), (192, 192))
PARTS = (PART_A,) + PART_B
MESH = pl.DeviceIdType.MESH
F32 = jnp.float32
BF16 = jnp.bfloat16


class Move:
    def __init__(self, src, dst, dz, dy, valid):
        self.src, self.dst, self.dz, self.dy, self.valid = src, dst, dz, dy, valid


class Exchange:
    def __init__(self, moves, send_sem, recv_sem):
        self.moves, self.send_sem, self.recv_sem = moves, send_sem, recv_sem
        self.order = {name: i for i, name in enumerate(moves)}
        position = lax.axis_index("ctx")
        self.z = lax.div(position, NY)
        self.y = lax.rem(position, NY)

    def at(self, dz, dy):
        return lax.rem(self.z + dz + NZ, NZ), lax.rem(self.y + dy + NY, NY)

    def index(self, dz, dy):
        z, y = self.at(dz, dy)
        return z * NY + y

    def sends(self, name):
        return self.moves[name].valid(self.z, self.y)

    def receives(self, name):
        move = self.moves[name]
        return move.valid(*self.at(-move.dz, -move.dy))

    def barrier(self):
        barrier = pltpu.get_barrier_semaphore()
        groups = {}
        for name, move in self.moves.items():
            groups.setdefault((move.dz, move.dy), []).append(name)
        waits = jnp.int32(0)
        for (dz, dy), names in groups.items():
            out, into = self.sends(names[0]), self.receives(names[0])
            for name in names[1:]:
                out, into = out | self.sends(name), into | self.receives(name)
            waits = waits + out.astype(jnp.int32)

            @pl.when(into)
            def _():
                pl.semaphore_signal(
                    barrier, inc=1, device_id={"ctx": self.index(-dz, -dy)}, device_id_type=MESH
                )

        pl.semaphore_wait(barrier, waits)

    def copy(self, name):
        move, i = self.moves[name], self.order[name]
        return pltpu.make_async_remote_copy(
            src_ref=move.src,
            dst_ref=move.dst,
            send_sem=self.send_sem.at[i],
            recv_sem=self.recv_sem.at[i],
            device_id={"ctx": self.index(move.dz, move.dy)},
            device_id_type=MESH,
        )

    def start(self, name):
        @pl.when(self.sends(name))
        def _():
            self.copy(name).start()

    def wait(self, name):
        @pl.when(self.receives(name))
        def _():
            self.copy(name).wait_recv()

    def finish(self):
        for name in self.moves:

            @pl.when(self.sends(name))
            def _():
                self.copy(name).wait_send()


def rows(ref, part, lead=None):
    window = pl.ds(part[0], part[1])
    return ref.at[window] if lead is None else ref.at[lead, window]


def outward_moves(own, cand, passed):
    moves = {}
    for i, part in enumerate(PARTS):
        mine, l4, l5 = rows(own, part), rows(cand, part, 4), rows(cand, part, 5)
        l6, l7 = rows(cand, part, 6), rows(cand, part, 7)
        moves["out one", i] = Move(mine, l4, 1, 0, lambda z, y: z < 15)
        moves["out two", i] = Move(l4, l5, 1, 0, lambda z, y: (z >= 1) & (z < 15))
        moves["out four", i] = Move(l5, l6, 2, 0, lambda z, y: (z >= 2) & (z < 14))
        if i == 0:
            moves["out eight", i] = Move(l6, l7, 4, 0, lambda z, y: (z >= 4) & (z < 12))
        else:
            via = passed.at[i - 1]
            moves["out back", i] = Move(mine, via, -4, 0, lambda z, y: z < 8)
            moves["out on", i] = Move(via, l7, -4, 0, lambda z, y: (z < 4) | (z >= 12))
    for k in range(3):
        by = 2**k
        moves["out near", k] = Move(own, cand.at[k + 1], 0, by, lambda z, y, by=by: y + by < NY)
        moves["out cross", k] = Move(
            cand.at[4], cand.at[k + 1], 0, by, lambda z, y, by=by: (y + by >= NY) & (z >= 1)
        )
    return moves


def homeward_moves(pieces, r8, r4, r2, r1, t4, t2, t1, passed, far, near):
    moves = {}
    for i, part in enumerate(PARTS):
        p7 = rows(pieces, part, 6)
        if i == 0:
            moves["eight", i] = Move(p7, r8, -4, 0, lambda z, y: z >= 8)
            src = rows(t4, part)
        else:
            via, last = passed.at[i - 1], rows(far, part)
            moves["back", i] = Move(p7, via, 4, 0, lambda z, y: z >= 8)
            moves["on", i] = Move(via, last, 4, 0, lambda z, y: (z < 4) | (z >= 12))
            src = rows(pieces, part, 5)
        moves["four", i] = Move(src, rows(r4, part), -2, 0, lambda z, y: z >= 4)
        moves["two", i] = Move(rows(t2, part), rows(r2, part), -1, 0, lambda z, y: z >= 2)
        moves["one", i] = Move(rows(t1, part), rows(r1, part), -1, 0, lambda z, y: z >= 1)
    for k in range(3):
        by = 2**k
        moves["near", k] = Move(
            pieces.at[k], near.at[k], 0, -by, lambda z, y, by=by: (y >= by) | (z >= 1)
        )
    return moves


MOVES = 20 + 17
NT = (((1,), (1,)), ((), ()))
TN = (((0,), (0,)), ((), ()))


def dot(a, b, dims=(((1,), (0,)), ((), ()))):
    return lax.dot_general(a, b, dims, preferred_element_type=F32)


def kernel(
    mask_ref, q_hbm, lat_hbm, ku_hbm, vu_hbm, og_hbm, att_ref, gq_ref, gl_ref,
    q_ref, ku_ref, vu_ref, og_ref, cand, out_passed,
    qa, keys, values, rope, near_scores, near_dprobs, probs, dscores, pk, pv,
    share, pieces, own_grad, r8, r4, r2, r1, t4, t2, t1, passed, far, near,
    local_sem, send_sem, recv_sem,
):
    moves = outward_moves(lat_hbm, cand, out_passed)
    moves.update(homeward_moves(pieces, r8, r4, r2, r1, t4, t2, t1, passed, far, near))
    ex = Exchange(moves, send_sem, recv_sem)
    z, y = ex.z, ex.y
    local = {
        name: pltpu.make_async_copy(src, dst, local_sem.at[i])
        for i, (name, src, dst) in enumerate(
            (
                ("own", lat_hbm, cand.at[0]),
                ("q", q_hbm, q_ref),
                ("ku", ku_hbm, ku_ref),
                ("vu", vu_hbm, vu_ref),
                ("og", og_hbm, og_ref),
            )
        )
    }
    for copy in local.values():
        copy.start()

    position = lax.axis_index("ctx")
    first = (position >= 1) & (mask_ref[0, jnp.maximum(position - 1, 0)] == 1)
    found = jnp.int32(0)
    level_of = [jnp.int32(0), jnp.int32(0)]
    slot_of = {}
    for level in range(2, LEVELS):
        source = position - 2 ** (level - 1)
        linked = (source >= 0) & (mask_ref[0, jnp.maximum(source, 0)] == 1) & (found < 2)
        for j in range(2):
            level_of[j] = jnp.where(linked & (found == j), level, level_of[j])
        slot_of[level] = jnp.where(linked, found, 2)
        found = found + linked.astype(jnp.int32)
    scale = (NOPE + ROPE) ** -0.5
    no = -jnp.inf
    t = lax.broadcasted_iota(jnp.int32, (TOK, 2 * TOK), 0)
    s = lax.broadcasted_iota(jnp.int32, (TOK, 2 * TOK), 1)
    near_allowed = jnp.where(s < TOK, t, jnp.where(first, 2 * TOK, -1)) >= s
    far_bias = jnp.where(lax.broadcasted_iota(jnp.int32, (1, 2 * TOK), 1) < found * TOK, 0.0, no)

    def rope_rows(j, block):
        padded = jnp.concatenate([block, jnp.zeros((64, TOK), BF16)], axis=0)
        rope[j * TOK : (j + 1) * TOK, :] = padded.astype(F32).T.astype(BF16)

    def project(j, blocks):
        part = slice(j * TOK, j * TOK + blocks.shape[1])
        keys[part, :] = dot(blocks, ku_ref[...], TN).astype(BF16)
        values[part, :] = dot(blocks, vu_ref[...], TN).astype(BF16)

    def near_head(h):
        cols = slice(h * 128, (h + 1) * 128)
        k_h = jnp.concatenate([keys[: 2 * TOK, cols], rope[: 2 * TOK, :]], axis=1)
        scores = dot(qa[:, h * 256 : (h + 1) * 256], k_h, NT)
        near_scores[h] = jnp.where(near_allowed, scores, no)
        near_dprobs[h] = dot(og_ref[:, cols], values[: 2 * TOK, cols], NT)

    ex.barrier()
    for i in (1, 2):
        ex.start(("out back", i))
    for i in range(3):
        ex.start(("out one", i))
    for k in (2, 1, 0):
        ex.start(("out near", k))
    local["q"].wait()
    for h in range(HEADS):
        base = h * (NOPE + ROPE)
        qa[:, h * 256 : (h + 1) * 256] = jnp.concatenate(
            [q_ref[:, base : base + 192].astype(F32), jnp.zeros((TOK, 64), F32)], axis=1
        ).astype(BF16)
    for i in range(3):
        ex.wait(("out one", i))
        ex.start(("out two", i))
    for k in (2, 1, 0):
        ex.start(("out cross", k))
    for name in ("own", "ku", "vu", "og"):
        local[name].wait()
    project(0, cand[0, :LATENT])
    rope_rows(0, cand[0, LATENT:])
    for i in (1, 2):
        ex.wait(("out back", i))
        ex.start(("out on", i))
    for i in range(3):
        ex.wait(("out two", i))
        ex.start(("out four", i))
    ex.wait(("out near", 0))
    ex.wait(("out cross", 0))
    project(1, cand[1, :LATENT])
    rope_rows(1, cand[1, LATENT:])
    ex.wait(("out four", 0))
    ex.start(("out eight", 0))
    for h in range(HEADS):
        near_head(h)
    for i in (1, 2):
        ex.wait(("out four", i))
    for k in (1, 2):
        ex.wait(("out near", k))
        ex.wait(("out cross", k))
    ex.wait(("out eight", 0))
    for i in (1, 2):
        ex.wait(("out on", i))

    far_rows = slice(2 * TOK, 4 * TOK)
    two, three = cand[level_of[0]], cand[level_of[1]]
    project(2, jnp.concatenate([two[:LATENT], three[:LATENT]], axis=1))
    rope_rows(2, two[LATENT:])
    rope_rows(3, three[LATENT:])
    rope_sum = jnp.zeros((2 * TOK, 128), F32)
    for h in range(HEADS):
        cols = slice(h * 128, (h + 1) * 128)
        q_h = qa[:, h * 256 : (h + 1) * 256]
        g_h = og_ref[:, cols]
        k_h = jnp.concatenate([keys[far_rows, cols], rope[far_rows, :]], axis=1)
        scores = jnp.concatenate([near_scores[h], dot(q_h, k_h, NT) + far_bias], axis=1)
        peak = jnp.max(scores, axis=1, keepdims=True)
        powers = jnp.exp((scores - peak) * scale)
        prob = powers * (1.0 / jnp.sum(powers, axis=1, keepdims=True))
        dprobs = jnp.concatenate([near_dprobs[h], dot(g_h, values[far_rows, cols], NT)], axis=1)
        delta = jnp.sum(prob * dprobs, axis=1, keepdims=True)
        prob_bf = prob.astype(BF16)
        dscore = (prob * (dprobs - delta) * scale).astype(BF16)
        probs[h] = prob_bf
        dscores[h] = dscore
        dk = dot(dscore[:, 2 * TOK :], q_h, TN)
        pk[far_rows, cols] = dk[:, :128].astype(BF16)
        rope_sum = rope_sum + dk[:, 128:]
        pv[far_rows, cols] = dot(prob_bf[:, 2 * TOK :], g_h, TN).astype(BF16)
    share[2] = jnp.zeros((WIRE, 128), BF16)

    def lifted(part, tokens):
        grad = dot(ku_ref[part, :], pk[tokens, :], NT)
        return grad + dot(vu_ref[part, :], pv[tokens, :], NT)

    for i in (1, 2, 0):
        begin, end = PARTS[i][0], PARTS[i][0] + PARTS[i][1]
        grad = lifted(slice(begin, min(end, LATENT)), far_rows)
        for j in range(2):
            share[j, begin : min(end, LATENT), :] = grad[:, j * TOK : (j + 1) * TOK].astype(BF16)
            if i == 0:
                turned = rope_sum[j * TOK : (j + 1) * TOK].T
                share[j, LATENT:, :] = turned[:ROPE].astype(BF16)
        for level in (7, 6, 5, 4, 3, 2):
            pieces[level - 1, begin:end, :] = share[slot_of[level], begin:end, :]
        if i > 0:
            ex.start(("back", i))
            ex.start(("four", i))
        else:
            ex.start(("eight", 0))
    for k in (2, 1):
        ex.start(("near", k))

    def piece(level, part):
        return pieces[level - 1, part[0] : part[0] + part[1], :].astype(F32)

    def got(ref, part, valid):
        return jnp.where(valid, ref[part[0] : part[0] + part[1], :].astype(F32), 0.0)

    near_rows = slice(0, 2 * TOK)
    rope_sum = jnp.zeros((2 * TOK, 128), F32)
    for h in range(HEADS):
        cols = slice(h * 128, (h + 1) * 128)
        dk = dot(dscores[h, :, : 2 * TOK], qa[:, h * 256 : (h + 1) * 256], TN)
        pk[near_rows, cols] = dk[:, :128].astype(BF16)
        rope_sum = rope_sum + dk[:, 128:]
        pv[near_rows, cols] = dot(probs[h, :, : 2 * TOK], og_ref[:, cols], TN).astype(BF16)
    grad = lifted(slice(0, LATENT), near_rows)
    own_grad[:LATENT, :] = grad[:, :TOK]
    own_grad[LATENT:, :] = rope_sum[:TOK].T[:ROPE]
    pieces[0, :LATENT, :] = grad[:, TOK:].astype(BF16)
    pieces[0, LATENT:, :] = rope_sum[TOK:].T[:ROPE].astype(BF16)
    ex.start(("near", 0))

    ex.wait(("eight", 0))
    a0, a1 = PART_A[0], PART_A[0] + PART_A[1]
    t4[a0:a1, :] = (piece(6, PART_A) + jnp.where(z <= 11, r8[...].astype(F32), 0.0)).astype(BF16)
    ex.start(("four", 0))
    for i in (1, 2):
        ex.wait(("back", i))
        ex.start(("on", i))

    def forward_out(h):
        cols = slice(h * 128, (h + 1) * 128)
        base = h * (NOPE + ROPE)
        att_ref[:, cols] = dot(probs[h], values[:, cols]).astype(BF16)
        k_h = jnp.concatenate([keys[:, cols], rope[...]], axis=1)
        gq_ref[:, base : base + 192] = dot(dscores[h], k_h)[:, :192].astype(BF16)

    for i in (1, 2, 0):
        part = PARTS[i]
        ex.wait(("four", i))
        t2[part[0] : part[0] + part[1], :] = (
            piece(5, part) + got(r4, part, z <= 13)
        ).astype(BF16)
        ex.start(("two", i))
    for h in range(4):
        forward_out(h)
    for k in range(3):
        ex.wait(("near", k))
    for i in (1, 2, 0):
        part = PARTS[i]
        ex.wait(("two", i))
        total = piece(4, part) + got(r2, part, z <= 14)
        for k in range(3):
            total = total + got(near.at[k], part, y + 2**k >= NY)
        t1[part[0] : part[0] + part[1], :] = total.astype(BF16)
        ex.start(("one", i))
    for h in range(4, HEADS):
        forward_out(h)
    for i in (1, 2):
        ex.wait(("on", i))
    for i in (1, 2, 0):
        part = PARTS[i]
        ex.wait(("one", i))
        total = own_grad[part[0] : part[0] + part[1], :] + got(r1, part, z <= 14)
        for k in range(3):
            total = total + got(near.at[k], part, y + 2**k < NY)
        if i > 0:
            total = total + got(far, part, z < 8)
        gl_ref[part[0] : part[0] + part[1], :] = total.astype(BF16)
    ex.finish()


def on_device(queries, latents, key_up, value_up, link_mask, out_grad):
    vmem = pl.BlockSpec(memory_space=pltpu.VMEM)
    hbm = pl.BlockSpec(memory_space=pltpu.HBM)
    block = pltpu.VMEM((WIRE, 128), BF16)
    keyed = pltpu.VMEM((SLOTS * TOK, WIDTH), BF16)
    passed = pltpu.VMEM((2, 192, 128), BF16)
    attention, grad_queries, grad_latents = pl.pallas_call(
        kernel,
        out_shape=(
            jax.ShapeDtypeStruct((TOK, WIDTH), BF16),
            jax.ShapeDtypeStruct((TOK, HEADS * (NOPE + ROPE)), BF16),
            jax.ShapeDtypeStruct((WIRE, TOK), BF16),
        ),
        in_specs=[pl.BlockSpec(memory_space=pltpu.SMEM)] + [hbm] * 5,
        out_specs=(vmem,) * 3,
        scratch_shapes=[
            pltpu.VMEM((TOK, HEADS * (NOPE + ROPE)), BF16),
            pltpu.VMEM((LATENT, WIDTH), BF16),
            pltpu.VMEM((LATENT, WIDTH), BF16),
            pltpu.VMEM((TOK, WIDTH), BF16),
            pltpu.VMEM((LEVELS, WIRE, 128), BF16),
            passed,
            pltpu.VMEM((TOK, HEADS * 256), BF16),
            keyed,
            keyed,
            pltpu.VMEM((SLOTS * TOK, 128), BF16),
            pltpu.VMEM((HEADS, TOK, 2 * TOK), F32),
            pltpu.VMEM((HEADS, TOK, 2 * TOK), F32),
            pltpu.VMEM((HEADS, TOK, 4 * TOK), BF16),
            pltpu.VMEM((HEADS, TOK, 4 * TOK), BF16),
            keyed,
            keyed,
            pltpu.VMEM((3, WIRE, 128), BF16),
            pltpu.VMEM((LEVELS - 1, WIRE, 128), BF16),
            pltpu.VMEM((WIRE, 128), F32),
            pltpu.VMEM((192, 128), BF16),
            block, block, block, block, block, block,
            passed,
            block,
            pltpu.VMEM((3, WIRE, 128), BF16),
            pltpu.SemaphoreType.DMA((5,)),
            pltpu.SemaphoreType.DMA((MOVES,)),
            pltpu.SemaphoreType.DMA((MOVES,)),
        ],
        compiler_params=pltpu.CompilerParams(
            collective_id=0, has_side_effects=True, vmem_limit_bytes=60 * 2**20
        ),
        name="attend",
    )(link_mask, queries, latents.T, key_up, value_up, out_grad)
    return attention, grad_queries, grad_latents.T


def solution(mesh):
    split = P(("dp", "ctx"), None)
    return jax.shard_map(
        on_device,
        mesh=mesh,
        in_specs=(split, split, P(), P(), split, split),
        out_specs=(split, split, split),
        check_vma=False,
    )
```

```python
import jax
import jax.numpy as jnp
from jax import lax
from jax.experimental import pallas as pl
from jax.experimental.pallas import tpu as pltpu
from jax.sharding import PartitionSpec as P

HEADS = 8
NOPE = 128
ROPE = 64
LATENT = 512
SLOTS = 4
TOK = 128
NY = 8
NZ = 16
LEVELS = 8
WIDTH = HEADS * NOPE
WIRE = LATENT + ROPE
PART_A = (384, 192)
PART_B = ((0, 192), (192, 192))
PARTS = (PART_A,) + PART_B
MESH = pl.DeviceIdType.MESH
F32 = jnp.float32
BF16 = jnp.bfloat16


class Move:
    def __init__(self, src, dst, dz, dy, valid):
        self.src, self.dst, self.dz, self.dy, self.valid = src, dst, dz, dy, valid


class Exchange:
    def __init__(self, moves, send_sem, recv_sem):
        self.moves, self.send_sem, self.recv_sem = moves, send_sem, recv_sem
        self.order = {name: i for i, name in enumerate(moves)}
        position = lax.axis_index("ctx")
        self.z = lax.div(position, NY)
        self.y = lax.rem(position, NY)

    def at(self, dz, dy):
        return lax.rem(self.z + dz + NZ, NZ), lax.rem(self.y + dy + NY, NY)

    def index(self, dz, dy):
        z, y = self.at(dz, dy)
        return z * NY + y

    def sends(self, name):
        return self.moves[name].valid(self.z, self.y)

    def receives(self, name):
        move = self.moves[name]
        return move.valid(*self.at(-move.dz, -move.dy))

    def barrier(self):
        barrier = pltpu.get_barrier_semaphore()
        groups = {}
        for name, move in self.moves.items():
            groups.setdefault((move.dz, move.dy), []).append(name)
        waits = jnp.int32(0)
        for (dz, dy), names in groups.items():
            out, into = self.sends(names[0]), self.receives(names[0])
            for name in names[1:]:
                out, into = out | self.sends(name), into | self.receives(name)
            waits = waits + out.astype(jnp.int32)

            @pl.when(into)
            def _():
                pl.semaphore_signal(
                    barrier, inc=1, device_id={"ctx": self.index(-dz, -dy)}, device_id_type=MESH
                )

        pl.semaphore_wait(barrier, waits)

    def copy(self, name):
        move, i = self.moves[name], self.order[name]
        return pltpu.make_async_remote_copy(
            src_ref=move.src,
            dst_ref=move.dst,
            send_sem=self.send_sem.at[i],
            recv_sem=self.recv_sem.at[i],
            device_id={"ctx": self.index(move.dz, move.dy)},
            device_id_type=MESH,
        )

    def start(self, name):
        @pl.when(self.sends(name))
        def _():
            self.copy(name).start()

    def wait(self, name):
        @pl.when(self.receives(name))
        def _():
            self.copy(name).wait_recv()

    def finish(self):
        for name in self.moves:

            @pl.when(self.sends(name))
            def _():
                self.copy(name).wait_send()


def rows(ref, part, lead=None):
    window = pl.ds(part[0], part[1])
    return ref.at[window] if lead is None else ref.at[lead, window]


def outward_moves(own, cand, passed):
    moves = {}
    for i, part in enumerate(PARTS):
        mine, l4, l5 = rows(own, part), rows(cand, part, 4), rows(cand, part, 5)
        l6, l7 = rows(cand, part, 6), rows(cand, part, 7)
        moves["out one", i] = Move(mine, l4, 1, 0, lambda z, y: z < 15)
        moves["out two", i] = Move(l4, l5, 1, 0, lambda z, y: (z >= 1) & (z < 15))
        moves["out four", i] = Move(l5, l6, 2, 0, lambda z, y: (z >= 2) & (z < 14))
        if i == 0:
            moves["out eight", i] = Move(l6, l7, 4, 0, lambda z, y: (z >= 4) & (z < 12))
        else:
            via = passed.at[i - 1]
            moves["out back", i] = Move(mine, via, -4, 0, lambda z, y: z < 8)
            moves["out on", i] = Move(via, l7, -4, 0, lambda z, y: (z < 4) | (z >= 12))
    for k in range(3):
        by = 2**k
        moves["out near", k] = Move(own, cand.at[k + 1], 0, by, lambda z, y, by=by: y + by < NY)
        for i, part in enumerate(PARTS):
            moves["out cross", k, i] = Move(
                rows(cand, part, 4), rows(cand, part, k + 1), 0, by,
                lambda z, y, by=by: (y + by >= NY) & (z >= 1),
            )
    return moves


def homeward_moves(pieces, r8, r4, r2, r1, t4, t2, t1, passed, far, near):
    moves = {}
    for i, part in enumerate(PARTS):
        p7 = rows(pieces, part, 6)
        if i == 0:
            moves["eight", i] = Move(p7, r8, -4, 0, lambda z, y: z >= 8)
            src = rows(t4, part)
        else:
            via, last = passed.at[i - 1], rows(far, part)
            moves["back", i] = Move(p7, via, 4, 0, lambda z, y: z >= 8)
            moves["on", i] = Move(via, last, 4, 0, lambda z, y: (z < 4) | (z >= 12))
            src = rows(pieces, part, 5)
        moves["four", i] = Move(src, rows(r4, part), -2, 0, lambda z, y: z >= 4)
        moves["two", i] = Move(rows(t2, part), rows(r2, part), -1, 0, lambda z, y: z >= 2)
        moves["one", i] = Move(rows(t1, part), rows(r1, part), -1, 0, lambda z, y: z >= 1)
    for k in range(3):
        by = 2**k
        moves["near", k] = Move(
            pieces.at[k], near.at[k], 0, -by, lambda z, y, by=by: (y >= by) | (z >= 1)
        )
    return moves


MOVES = 26 + 17
NT = (((1,), (1,)), ((), ()))
TN = (((0,), (0,)), ((), ()))


def dot(a, b, dims=(((1,), (0,)), ((), ()))):
    return lax.dot_general(a, b, dims, preferred_element_type=F32)


def kernel(
    mask_ref, q_hbm, lat_hbm, ku_hbm, vu_hbm, og_hbm, att_ref, gq_ref, gl_ref,
    q_ref, ku_ref, vu_ref, og_ref, cand, out_passed,
    qa, keys, values, rope, near_powers, near_dprobs, near_peak, near_sum, near_dot, probs, dscores, pk, pv,
    share, pieces, own_grad, r8, r4, r2, r1, t4, t2, t1, passed, far, near,
    local_sem, send_sem, recv_sem,
):
    moves = outward_moves(lat_hbm, cand, out_passed)
    moves.update(homeward_moves(pieces, r8, r4, r2, r1, t4, t2, t1, passed, far, near))
    ex = Exchange(moves, send_sem, recv_sem)
    z, y = ex.z, ex.y
    local = {
        name: pltpu.make_async_copy(src, dst, local_sem.at[i])
        for i, (name, src, dst) in enumerate(
            (
                ("own", lat_hbm, cand.at[0]),
                ("q", q_hbm, q_ref),
                ("ku", ku_hbm, ku_ref),
                ("vu", vu_hbm, vu_ref),
                ("og", og_hbm, og_ref),
            )
        )
    }
    for copy in local.values():
        copy.start()

    position = lax.axis_index("ctx")
    first = (position >= 1) & (mask_ref[0, jnp.maximum(position - 1, 0)] == 1)
    found = jnp.int32(0)
    level_of = [jnp.int32(0), jnp.int32(0)]
    slot_of = {}
    for level in range(2, LEVELS):
        source = position - 2 ** (level - 1)
        linked = (source >= 0) & (mask_ref[0, jnp.maximum(source, 0)] == 1) & (found < 2)
        for j in range(2):
            level_of[j] = jnp.where(linked & (found == j), level, level_of[j])
        slot_of[level] = jnp.where(linked, found, 2)
        found = found + linked.astype(jnp.int32)
    scale = (NOPE + ROPE) ** -0.5
    no = -jnp.inf
    t = lax.broadcasted_iota(jnp.int32, (TOK, 2 * TOK), 0)
    s = lax.broadcasted_iota(jnp.int32, (TOK, 2 * TOK), 1)
    near_allowed = jnp.where(s < TOK, t, jnp.where(first, 2 * TOK, -1)) >= s
    far_bias = jnp.where(lax.broadcasted_iota(jnp.int32, (1, 2 * TOK), 1) < found * TOK, 0.0, no)

    def rope_rows(j, block):
        padded = jnp.concatenate([block, jnp.zeros((64, TOK), BF16)], axis=0)
        rope[j * TOK : (j + 1) * TOK, :] = padded.astype(F32).T.astype(BF16)

    def project(j, blocks):
        part = slice(j * TOK, j * TOK + blocks.shape[1])
        keys[part, :] = dot(blocks, ku_ref[...], TN).astype(BF16)
        values[part, :] = dot(blocks, vu_ref[...], TN).astype(BF16)

    def near_head(h):
        cols = slice(h * 128, (h + 1) * 128)
        k_h = jnp.concatenate([keys[: 2 * TOK, cols], rope[: 2 * TOK, :]], axis=1)
        scores = dot(qa[:, h * 256 : (h + 1) * 256], k_h, NT)
        scores = jnp.where(near_allowed, scores, no)
        peak = jnp.max(scores, axis=1, keepdims=True)
        powers = jnp.exp((scores - peak) * scale)
        dprobs = dot(og_ref[:, cols], values[: 2 * TOK, cols], NT)
        near_powers[h] = powers
        near_dprobs[h] = dprobs
        near_peak[h] = peak
        near_sum[h] = jnp.sum(powers, axis=1, keepdims=True)
        near_dot[h] = jnp.sum(powers * dprobs, axis=1, keepdims=True)

    def from_y(k):
        ex.wait(("out near", k))
        for i in range(3):
            ex.wait(("out cross", k, i))

    ex.barrier()
    for i in (1, 2):
        ex.start(("out back", i))
    for i in range(3):
        ex.start(("out one", i))
    local["q"].wait()
    for h in range(HEADS):
        base = h * (NOPE + ROPE)
        qa[:, h * 256 : (h + 1) * 256] = jnp.concatenate(
            [q_ref[:, base : base + 192].astype(F32), jnp.zeros((TOK, 64), F32)], axis=1
        ).astype(BF16)
    for i in range(3):
        ex.wait(("out one", i))
        ex.start(("out two", i))
        for k in (2, 1, 0):
            ex.start(("out cross", k, i))
    for k in (0, 2, 1):
        ex.start(("out near", k))
    for name in ("own", "ku", "vu", "og"):
        local[name].wait()
    project(0, cand[0, :LATENT])
    rope_rows(0, cand[0, LATENT:])
    for i in (1, 2):
        ex.wait(("out back", i))
        ex.start(("out on", i))
    for i in range(3):
        ex.wait(("out two", i))
        ex.start(("out four", i))
    ex.wait(("out four", 0))
    ex.start(("out eight", 0))
    from_y(0)
    project(1, cand[1, :LATENT])
    rope_rows(1, cand[1, LATENT:])
    for h in range(HEADS):
        near_head(h)
    for i in (1, 2):
        ex.wait(("out four", i))
    for k in (1, 2):
        from_y(k)
    ex.wait(("out eight", 0))
    for i in (1, 2):
        ex.wait(("out on", i))

    far_rows = slice(2 * TOK, 4 * TOK)
    two, three = cand[level_of[0]], cand[level_of[1]]
    project(2, jnp.concatenate([two[:LATENT], three[:LATENT]], axis=1))
    rope_rows(2, two[LATENT:])
    rope_rows(3, three[LATENT:])
    rope_sum = jnp.zeros((2 * TOK, 128), F32)
    for h in range(HEADS):
        cols = slice(h * 128, (h + 1) * 128)
        q_h = qa[:, h * 256 : (h + 1) * 256]
        g_h = og_ref[:, cols]
        k_h = jnp.concatenate([keys[far_rows, cols], rope[far_rows, :]], axis=1)
        scores = dot(q_h, k_h, NT) + far_bias
        peak = jnp.maximum(near_peak[h], jnp.max(scores, axis=1, keepdims=True))
        powers = jnp.exp((scores - peak) * scale)
        near_factor = jnp.exp((near_peak[h] - peak) * scale)
        inverse = 1.0 / (near_factor * near_sum[h] + jnp.sum(powers, axis=1, keepdims=True))
        near_factor = near_factor * inverse
        prob = powers * inverse
        dprobs = dot(g_h, values[far_rows, cols], NT)
        delta = near_factor * near_dot[h] + jnp.sum(prob * dprobs, axis=1, keepdims=True)
        prob_bf = prob.astype(BF16)
        dscore = (prob * (dprobs - delta) * scale).astype(BF16)
        probs[h, :, 2 * TOK :] = prob_bf
        dscores[h, :, 2 * TOK :] = dscore
        near_sum[h] = near_factor
        near_dot[h] = delta
        dk = dot(dscore, q_h, TN)
        pk[far_rows, cols] = dk[:, :128].astype(BF16)
        rope_sum = rope_sum + dk[:, 128:]
        pv[far_rows, cols] = dot(prob_bf, g_h, TN).astype(BF16)
    share[2] = jnp.zeros((WIRE, 128), BF16)

    def lifted(part, tokens):
        grad = dot(ku_ref[part, :], pk[tokens, :], NT)
        return grad + dot(vu_ref[part, :], pv[tokens, :], NT)

    for i in (1, 2, 0):
        begin, end = PARTS[i][0], PARTS[i][0] + PARTS[i][1]
        grad = lifted(slice(begin, min(end, LATENT)), far_rows)
        for j in range(2):
            share[j, begin : min(end, LATENT), :] = grad[:, j * TOK : (j + 1) * TOK].astype(BF16)
            if i == 0:
                turned = rope_sum[j * TOK : (j + 1) * TOK].T
                share[j, LATENT:, :] = turned[:ROPE].astype(BF16)
        for level in (7, 6, 5, 4, 3, 2):
            pieces[level - 1, begin:end, :] = share[slot_of[level], begin:end, :]
        if i > 0:
            ex.start(("back", i))
            ex.start(("four", i))
        else:
            ex.start(("eight", 0))
    for k in (2, 1):
        ex.start(("near", k))

    def piece(level, part):
        return pieces[level - 1, part[0] : part[0] + part[1], :].astype(F32)

    def got(ref, part, valid):
        return jnp.where(valid, ref[part[0] : part[0] + part[1], :].astype(F32), 0.0)

    near_rows = slice(0, 2 * TOK)
    rope_sum = jnp.zeros((2 * TOK, 128), F32)
    for h in range(HEADS):
        cols = slice(h * 128, (h + 1) * 128)
        prob = near_powers[h] * near_sum[h]
        prob_bf = prob.astype(BF16)
        dscore = (prob * (near_dprobs[h] - near_dot[h]) * scale).astype(BF16)
        probs[h, :, : 2 * TOK] = prob_bf
        dscores[h, :, : 2 * TOK] = dscore
        dk = dot(dscore, qa[:, h * 256 : (h + 1) * 256], TN)
        pk[near_rows, cols] = dk[:, :128].astype(BF16)
        rope_sum = rope_sum + dk[:, 128:]
        pv[near_rows, cols] = dot(prob_bf, og_ref[:, cols], TN).astype(BF16)
    grad = lifted(slice(0, LATENT), near_rows)
    own_grad[:LATENT, :] = grad[:, :TOK]
    own_grad[LATENT:, :] = rope_sum[:TOK].T[:ROPE]
    pieces[0, :LATENT, :] = grad[:, TOK:].astype(BF16)
    pieces[0, LATENT:, :] = rope_sum[TOK:].T[:ROPE].astype(BF16)
    ex.start(("near", 0))

    ex.wait(("eight", 0))
    a0, a1 = PART_A[0], PART_A[0] + PART_A[1]
    t4[a0:a1, :] = (piece(6, PART_A) + jnp.where(z <= 11, r8[...].astype(F32), 0.0)).astype(BF16)
    ex.start(("four", 0))
    for i in (1, 2):
        ex.wait(("back", i))
        ex.start(("on", i))

    def forward_out(h):
        cols = slice(h * 128, (h + 1) * 128)
        base = h * (NOPE + ROPE)
        att_ref[:, cols] = dot(probs[h], values[:, cols]).astype(BF16)
        k_h = jnp.concatenate([keys[:, cols], rope[...]], axis=1)
        gq_ref[:, base : base + 192] = dot(dscores[h], k_h)[:, :192].astype(BF16)

    for i in (1, 2, 0):
        part = PARTS[i]
        ex.wait(("four", i))
        t2[part[0] : part[0] + part[1], :] = (
            piece(5, part) + got(r4, part, z <= 13)
        ).astype(BF16)
        ex.start(("two", i))
    for h in range(4):
        forward_out(h)
    for k in range(3):
        ex.wait(("near", k))
    for i in (1, 2, 0):
        part = PARTS[i]
        ex.wait(("two", i))
        total = piece(4, part) + got(r2, part, z <= 14)
        for k in range(3):
            total = total + got(near.at[k], part, y + 2**k >= NY)
        t1[part[0] : part[0] + part[1], :] = total.astype(BF16)
        ex.start(("one", i))
    for h in range(4, HEADS):
        forward_out(h)
    for i in (1, 2):
        ex.wait(("on", i))
    for i in (1, 2, 0):
        part = PARTS[i]
        ex.wait(("one", i))
        total = own_grad[part[0] : part[0] + part[1], :] + got(r1, part, z <= 14)
        for k in range(3):
            total = total + got(near.at[k], part, y + 2**k < NY)
        if i > 0:
            total = total + got(far, part, z < 8)
        gl_ref[part[0] : part[0] + part[1], :] = total.astype(BF16)
    ex.finish()


def hand_over_kernel(*refs):
    sources, targets, held, sem = refs[:3], refs[3:6], refs[6:9], refs[9]
    into = [pltpu.make_async_copy(sources[i], held[i], sem.at[i]) for i in range(3)]
    out = [pltpu.make_async_copy(held[i], targets[i], sem.at[3 + i]) for i in range(3)]
    for copy in into:
        copy.start()
    for i in range(3):
        into[i].wait()
        out[i].start()
    for copy in out:
        copy.wait()


def hand_over(*arrays):
    hbm = pl.BlockSpec(memory_space=pltpu.HBM)
    return pl.pallas_call(
        hand_over_kernel,
        out_shape=tuple(jax.ShapeDtypeStruct(a.shape, a.dtype) for a in arrays),
        in_specs=[hbm] * 3,
        out_specs=(hbm,) * 3,
        scratch_shapes=[pltpu.VMEM(a.shape, a.dtype) for a in arrays] + [pltpu.SemaphoreType.DMA((6,))],
        compiler_params=pltpu.CompilerParams(vmem_limit_bytes=60 * 2**20),
        name="hand_over",
    )(*arrays)


def on_device(queries, latents, key_up, value_up, link_mask, out_grad):
    vmem = pl.BlockSpec(memory_space=pltpu.VMEM)
    hbm = pl.BlockSpec(memory_space=pltpu.HBM)
    block = pltpu.VMEM((WIRE, 128), BF16)
    keyed = pltpu.VMEM((SLOTS * TOK, WIDTH), BF16)
    passed = pltpu.VMEM((2, 192, 128), BF16)
    attention, grad_queries, grad_latents = pl.pallas_call(
        kernel,
        out_shape=(
            jax.ShapeDtypeStruct((TOK, WIDTH), BF16),
            jax.ShapeDtypeStruct((TOK, HEADS * (NOPE + ROPE)), BF16),
            jax.ShapeDtypeStruct((WIRE, TOK), BF16),
        ),
        in_specs=[pl.BlockSpec(memory_space=pltpu.SMEM)] + [hbm] * 5,
        out_specs=(vmem,) * 3,
        scratch_shapes=[
            pltpu.VMEM((TOK, HEADS * (NOPE + ROPE)), BF16),
            pltpu.VMEM((LATENT, WIDTH), BF16),
            pltpu.VMEM((LATENT, WIDTH), BF16),
            pltpu.VMEM((TOK, WIDTH), BF16),
            pltpu.VMEM((LEVELS, WIRE, 128), BF16),
            passed,
            pltpu.VMEM((TOK, HEADS * 256), BF16),
            keyed,
            keyed,
            pltpu.VMEM((SLOTS * TOK, 128), BF16),
            pltpu.VMEM((HEADS, TOK, 2 * TOK), F32),
            pltpu.VMEM((HEADS, TOK, 2 * TOK), F32),
            pltpu.VMEM((HEADS, TOK, 1), F32),
            pltpu.VMEM((HEADS, TOK, 1), F32),
            pltpu.VMEM((HEADS, TOK, 1), F32),
            pltpu.VMEM((HEADS, TOK, 4 * TOK), BF16),
            pltpu.VMEM((HEADS, TOK, 4 * TOK), BF16),
            keyed,
            keyed,
            pltpu.VMEM((3, WIRE, 128), BF16),
            pltpu.VMEM((LEVELS - 1, WIRE, 128), BF16),
            pltpu.VMEM((WIRE, 128), F32),
            pltpu.VMEM((192, 128), BF16),
            block, block, block, block, block, block,
            passed,
            block,
            pltpu.VMEM((3, WIRE, 128), BF16),
            pltpu.SemaphoreType.DMA((5,)),
            pltpu.SemaphoreType.DMA((MOVES,)),
            pltpu.SemaphoreType.DMA((MOVES,)),
        ],
        compiler_params=pltpu.CompilerParams(
            collective_id=0, has_side_effects=True, vmem_limit_bytes=60 * 2**20
        ),
        name="attend",
    )(link_mask, queries, latents.T, key_up, value_up, out_grad)
    attention, grad_queries, grad_latents = hand_over(attention, grad_queries, grad_latents)
    return attention, grad_queries, grad_latents.T


def solution(mesh):
    split = P(("dp", "ctx"), None)
    return jax.shard_map(
        on_device,
        mesh=mesh,
        in_specs=(split, split, P(), P(), split, split),
        out_specs=(split, split, split),
        check_vma=False,
    )
```

```python
import jax
import jax.numpy as jnp
from jax import lax
from jax.experimental import pallas as pl
from jax.experimental.pallas import tpu as pltpu
from jax.sharding import PartitionSpec as P

HEADS = 8
NOPE = 128
ROPE = 64
LATENT = 512
SLOTS = 4
TOK = 128
NY = 8
NZ = 16
LEVELS = 8
WIDTH = HEADS * NOPE
WIRE = LATENT + ROPE
PART_A = (384, 192)
PART_B = ((0, 192), (192, 192))
PARTS = (PART_A,) + PART_B
MESH = pl.DeviceIdType.MESH
F32 = jnp.float32
BF16 = jnp.bfloat16


class Move:
    def __init__(self, src, dst, dz, dy, valid):
        self.src, self.dst, self.dz, self.dy, self.valid = src, dst, dz, dy, valid


class Exchange:
    def __init__(self, moves, send_sem, recv_sem):
        self.moves, self.send_sem, self.recv_sem = moves, send_sem, recv_sem
        self.order = {name: i for i, name in enumerate(moves)}
        position = lax.axis_index("ctx")
        self.z = lax.div(position, NY)
        self.y = lax.rem(position, NY)

    def at(self, dz, dy):
        return lax.rem(self.z + dz + NZ, NZ), lax.rem(self.y + dy + NY, NY)

    def index(self, dz, dy):
        z, y = self.at(dz, dy)
        return z * NY + y

    def sends(self, name):
        return self.moves[name].valid(self.z, self.y)

    def receives(self, name):
        move = self.moves[name]
        return move.valid(*self.at(-move.dz, -move.dy))

    def barrier(self):
        barrier = pltpu.get_barrier_semaphore()
        groups = {}
        for name, move in self.moves.items():
            groups.setdefault((move.dz, move.dy), []).append(name)
        waits = jnp.int32(0)
        for (dz, dy), names in groups.items():
            out, into = self.sends(names[0]), self.receives(names[0])
            for name in names[1:]:
                out, into = out | self.sends(name), into | self.receives(name)
            waits = waits + out.astype(jnp.int32)

            @pl.when(into)
            def _():
                pl.semaphore_signal(
                    barrier, inc=1, device_id={"ctx": self.index(-dz, -dy)}, device_id_type=MESH
                )

        pl.semaphore_wait(barrier, waits)

    def copy(self, name):
        move, i = self.moves[name], self.order[name]
        return pltpu.make_async_remote_copy(
            src_ref=move.src,
            dst_ref=move.dst,
            send_sem=self.send_sem.at[i],
            recv_sem=self.recv_sem.at[i],
            device_id={"ctx": self.index(move.dz, move.dy)},
            device_id_type=MESH,
        )

    def start(self, name):
        @pl.when(self.sends(name))
        def _():
            self.copy(name).start()

    def wait(self, name):
        @pl.when(self.receives(name))
        def _():
            self.copy(name).wait_recv()

    def finish(self):
        for name in self.moves:

            @pl.when(self.sends(name))
            def _():
                self.copy(name).wait_send()


def rows(ref, part, lead=None):
    window = pl.ds(part[0], part[1])
    return ref.at[window] if lead is None else ref.at[lead, window]


def outward_moves(own, cand, passed):
    moves = {}
    for i, part in enumerate(PARTS):
        mine, l4, l5 = rows(own, part), rows(cand, part, 4), rows(cand, part, 5)
        l6, l7 = rows(cand, part, 6), rows(cand, part, 7)
        moves["out one", i] = Move(mine, l4, 1, 0, lambda z, y: z < 15)
        moves["out two", i] = Move(l4, l5, 1, 0, lambda z, y: (z >= 1) & (z < 15))
        moves["out four", i] = Move(l5, l6, 2, 0, lambda z, y: (z >= 2) & (z < 14))
        if i == 0:
            moves["out eight", i] = Move(l6, l7, 4, 0, lambda z, y: (z >= 4) & (z < 12))
        else:
            via = passed.at[i - 1]
            moves["out back", i] = Move(mine, via, -4, 0, lambda z, y: z < 8)
            moves["out on", i] = Move(via, l7, -4, 0, lambda z, y: (z < 4) | (z >= 12))
    for k in range(3):
        by = 2**k
        moves["out near", k] = Move(own, cand.at[k + 1], 0, by, lambda z, y, by=by: y + by < NY)
        for i, part in enumerate(PARTS):
            moves["out cross", k, i] = Move(
                rows(cand, part, 4), rows(cand, part, k + 1), 0, by,
                lambda z, y, by=by: (y + by >= NY) & (z >= 1),
            )
    return moves


def homeward_moves(pieces, r8, r4, r2, r1, t4, t2, t1, passed, far, near, cross):
    moves = {}
    for i, part in enumerate(PARTS):
        p7 = rows(pieces, part, 6)
        if i == 0:
            moves["eight", i] = Move(p7, r8, -4, 0, lambda z, y: z >= 8)
            src = rows(t4, part)
        else:
            via, last = passed.at[i - 1], rows(far, part)
            moves["back", i] = Move(p7, via, 4, 0, lambda z, y: z >= 8)
            moves["on", i] = Move(via, last, 4, 0, lambda z, y: (z < 4) | (z >= 12))
            src = rows(pieces, part, 5)
        moves["four", i] = Move(src, rows(r4, part), -2, 0, lambda z, y: z >= 4)
        moves["two", i] = Move(rows(t2, part), rows(r2, part), -1, 0, lambda z, y: z >= 2)
        moves["one", i] = Move(rows(t1, part), rows(r1, part), -1, 0, lambda z, y: z >= 1)
    for k in range(3):
        by = 2**k
        moves["near", k] = Move(
            pieces.at[k], near.at[k], 0, -by, lambda z, y, by=by: y >= by
        )
        moves["cross", k] = Move(
            pieces.at[k], cross.at[k], 0, -by, lambda z, y, by=by: (y < by) & (z >= 1)
        )
    return moves


MOVES = 26 + 20
NT = (((1,), (1,)), ((), ()))
TN = (((0,), (0,)), ((), ()))


def dot(a, b, dims=(((1,), (0,)), ((), ()))):
    return lax.dot_general(a, b, dims, preferred_element_type=F32)


def kernel(
    mask_ref, q_hbm, lat_hbm, ku_hbm, vu_hbm, og_hbm, att_ref, gq_ref, gl_ref,
    q_ref, ku_ref, vu_ref, og_ref, cand, out_passed,
    qa, keys, values, rope, near_powers, near_dprobs, near_peak, near_sum, near_dot, probs, dscores, pk, pv,
    share, pieces, own_grad, r8, r4, r2, r1, t4, t2, t1, passed, far, near, cross,
    local_sem, send_sem, recv_sem,
):
    moves = outward_moves(lat_hbm, cand, out_passed)
    moves.update(homeward_moves(pieces, r8, r4, r2, r1, t4, t2, t1, passed, far, near, cross))
    ex = Exchange(moves, send_sem, recv_sem)
    z, y = ex.z, ex.y
    local = {
        name: pltpu.make_async_copy(src, dst, local_sem.at[i])
        for i, (name, src, dst) in enumerate(
            (
                ("own", lat_hbm, cand.at[0]),
                ("q", q_hbm, q_ref),
                ("ku", ku_hbm, ku_ref),
                ("vu", vu_hbm, vu_ref),
                ("og", og_hbm, og_ref),
            )
        )
    }
    for copy in local.values():
        copy.start()

    position = lax.axis_index("ctx")
    first = (position >= 1) & (mask_ref[0, jnp.maximum(position - 1, 0)] == 1)
    found = jnp.int32(0)
    level_of = [jnp.int32(0), jnp.int32(0)]
    slot_of = {}
    for level in range(2, LEVELS):
        source = position - 2 ** (level - 1)
        linked = (source >= 0) & (mask_ref[0, jnp.maximum(source, 0)] == 1) & (found < 2)
        for j in range(2):
            level_of[j] = jnp.where(linked & (found == j), level, level_of[j])
        slot_of[level] = jnp.where(linked, found, 2)
        found = found + linked.astype(jnp.int32)
    scale = (NOPE + ROPE) ** -0.5
    no = -jnp.inf
    t = lax.broadcasted_iota(jnp.int32, (TOK, 2 * TOK), 0)
    s = lax.broadcasted_iota(jnp.int32, (TOK, 2 * TOK), 1)
    near_allowed = jnp.where(s < TOK, t, jnp.where(first, 2 * TOK, -1)) >= s
    far_bias = jnp.where(lax.broadcasted_iota(jnp.int32, (1, 2 * TOK), 1) < found * TOK, 0.0, no)

    def rope_rows(j, block):
        padded = jnp.concatenate([block, jnp.zeros((64, TOK), BF16)], axis=0)
        rope[j * TOK : (j + 1) * TOK, :] = padded.astype(F32).T.astype(BF16)

    def project(j, blocks):
        part = slice(j * TOK, j * TOK + blocks.shape[1])
        keys[part, :] = dot(blocks, ku_ref[...], TN).astype(BF16)
        values[part, :] = dot(blocks, vu_ref[...], TN).astype(BF16)

    def near_head(h):
        cols = slice(h * 128, (h + 1) * 128)
        k_h = jnp.concatenate([keys[: 2 * TOK, cols], rope[: 2 * TOK, :]], axis=1)
        scores = dot(qa[:, h * 256 : (h + 1) * 256], k_h, NT)
        scores = jnp.where(near_allowed, scores, no)
        peak = jnp.max(scores, axis=1, keepdims=True)
        powers = jnp.exp((scores - peak) * scale)
        dprobs = dot(og_ref[:, cols], values[: 2 * TOK, cols], NT)
        near_powers[h] = powers
        near_dprobs[h] = dprobs
        near_peak[h] = peak
        near_sum[h] = jnp.sum(powers, axis=1, keepdims=True)
        near_dot[h] = jnp.sum(powers * dprobs, axis=1, keepdims=True)

    def from_y(k):
        ex.wait(("out near", k))
        for i in range(3):
            ex.wait(("out cross", k, i))

    ex.barrier()
    for i in (1, 2):
        ex.start(("out back", i))
    for i in range(3):
        ex.start(("out one", i))
    local["q"].wait()
    for h in range(HEADS):
        base = h * (NOPE + ROPE)
        qa[:, h * 256 : (h + 1) * 256] = jnp.concatenate(
            [q_ref[:, base : base + 192].astype(F32), jnp.zeros((TOK, 64), F32)], axis=1
        ).astype(BF16)
    for i in range(3):
        ex.wait(("out one", i))
        ex.start(("out two", i))
        for k in (2, 1, 0):
            ex.start(("out cross", k, i))
    for k in (0, 2, 1):
        ex.start(("out near", k))
    for name in ("own", "ku", "vu", "og"):
        local[name].wait()
    project(0, cand[0, :LATENT])
    rope_rows(0, cand[0, LATENT:])
    for i in (1, 2):
        ex.wait(("out back", i))
        ex.start(("out on", i))
    for i in range(3):
        ex.wait(("out two", i))
        ex.start(("out four", i))
    ex.wait(("out four", 0))
    ex.start(("out eight", 0))
    from_y(0)
    project(1, cand[1, :LATENT])
    rope_rows(1, cand[1, LATENT:])
    for h in range(HEADS):
        near_head(h)
    for i in (1, 2):
        ex.wait(("out four", i))
    for k in (1, 2):
        from_y(k)
    ex.wait(("out eight", 0))
    for i in (1, 2):
        ex.wait(("out on", i))

    far_rows = slice(2 * TOK, 4 * TOK)
    two, three = cand[level_of[0]], cand[level_of[1]]
    project(2, jnp.concatenate([two[:LATENT], three[:LATENT]], axis=1))
    rope_rows(2, two[LATENT:])
    rope_rows(3, three[LATENT:])
    rope_sum = jnp.zeros((2 * TOK, 128), F32)
    for h in range(HEADS):
        cols = slice(h * 128, (h + 1) * 128)
        q_h = qa[:, h * 256 : (h + 1) * 256]
        g_h = og_ref[:, cols]
        k_h = jnp.concatenate([keys[far_rows, cols], rope[far_rows, :]], axis=1)
        scores = dot(q_h, k_h, NT) + far_bias
        peak = jnp.maximum(near_peak[h], jnp.max(scores, axis=1, keepdims=True))
        powers = jnp.exp((scores - peak) * scale)
        near_factor = jnp.exp((near_peak[h] - peak) * scale)
        inverse = 1.0 / (near_factor * near_sum[h] + jnp.sum(powers, axis=1, keepdims=True))
        near_factor = near_factor * inverse
        prob = powers * inverse
        dprobs = dot(g_h, values[far_rows, cols], NT)
        delta = near_factor * near_dot[h] + jnp.sum(prob * dprobs, axis=1, keepdims=True)
        prob_bf = prob.astype(BF16)
        dscore = (prob * (dprobs - delta) * scale).astype(BF16)
        probs[h, :, 2 * TOK :] = prob_bf
        dscores[h, :, 2 * TOK :] = dscore
        near_sum[h] = near_factor
        near_dot[h] = delta
        dk = dot(dscore, q_h, TN)
        pk[far_rows, cols] = dk[:, :128].astype(BF16)
        rope_sum = rope_sum + dk[:, 128:]
        pv[far_rows, cols] = dot(prob_bf, g_h, TN).astype(BF16)
    share[2] = jnp.zeros((WIRE, 128), BF16)

    def lifted(part, tokens):
        grad = dot(ku_ref[part, :], pk[tokens, :], NT)
        return grad + dot(vu_ref[part, :], pv[tokens, :], NT)

    for i in (1, 2, 0):
        begin, end = PARTS[i][0], PARTS[i][0] + PARTS[i][1]
        grad = lifted(slice(begin, min(end, LATENT)), far_rows)
        for j in range(2):
            share[j, begin : min(end, LATENT), :] = grad[:, j * TOK : (j + 1) * TOK].astype(BF16)
            if i == 0:
                turned = rope_sum[j * TOK : (j + 1) * TOK].T
                share[j, LATENT:, :] = turned[:ROPE].astype(BF16)
        for level in (7, 6, 5, 4, 3, 2):
            pieces[level - 1, begin:end, :] = share[slot_of[level], begin:end, :]
        if i > 0:
            ex.start(("back", i))
            ex.start(("four", i))
        else:
            ex.start(("eight", 0))
    for k in (2, 1):
        ex.start(("cross", k))
        ex.start(("near", k))

    def piece(level, part):
        return pieces[level - 1, part[0] : part[0] + part[1], :].astype(F32)

    def got(ref, part, valid):
        return jnp.where(valid, ref[part[0] : part[0] + part[1], :].astype(F32), 0.0)

    near_rows = slice(0, 2 * TOK)
    rope_sum = jnp.zeros((2 * TOK, 128), F32)
    for h in range(HEADS):
        cols = slice(h * 128, (h + 1) * 128)
        prob = near_powers[h] * near_sum[h]
        prob_bf = prob.astype(BF16)
        dscore = (prob * (near_dprobs[h] - near_dot[h]) * scale).astype(BF16)
        probs[h, :, : 2 * TOK] = prob_bf
        dscores[h, :, : 2 * TOK] = dscore
        dk = dot(dscore, qa[:, h * 256 : (h + 1) * 256], TN)
        pk[near_rows, cols] = dk[:, :128].astype(BF16)
        rope_sum = rope_sum + dk[:, 128:]
        pv[near_rows, cols] = dot(prob_bf, og_ref[:, cols], TN).astype(BF16)
    grad = lifted(slice(0, LATENT), near_rows)
    own_grad[:LATENT, :] = grad[:, :TOK]
    own_grad[LATENT:, :] = rope_sum[:TOK].T[:ROPE]
    pieces[0, :LATENT, :] = grad[:, TOK:].astype(BF16)
    pieces[0, LATENT:, :] = rope_sum[TOK:].T[:ROPE].astype(BF16)
    ex.start(("cross", 0))
    ex.start(("near", 0))

    ex.wait(("eight", 0))
    a0, a1 = PART_A[0], PART_A[0] + PART_A[1]
    t4[a0:a1, :] = (piece(6, PART_A) + jnp.where(z <= 11, r8[...].astype(F32), 0.0)).astype(BF16)
    ex.start(("four", 0))
    for i in (1, 2):
        ex.wait(("back", i))
        ex.start(("on", i))

    def forward_out(h):
        cols = slice(h * 128, (h + 1) * 128)
        base = h * (NOPE + ROPE)
        att_ref[:, cols] = dot(probs[h], values[:, cols]).astype(BF16)
        k_h = jnp.concatenate([keys[:, cols], rope[...]], axis=1)
        gq_ref[:, base : base + 192] = dot(dscores[h], k_h)[:, :192].astype(BF16)

    for i in (1, 2, 0):
        part = PARTS[i]
        ex.wait(("four", i))
        t2[part[0] : part[0] + part[1], :] = (
            piece(5, part) + got(r4, part, z <= 13)
        ).astype(BF16)
        ex.start(("two", i))
    for h in range(4):
        forward_out(h)
    for k in range(3):
        ex.wait(("cross", k))
    for i in (1, 2, 0):
        part = PARTS[i]
        ex.wait(("two", i))
        total = piece(4, part) + got(r2, part, z <= 14)
        for k in range(3):
            total = total + got(cross.at[k], part, (y + 2**k >= NY) & (z >= 1))
        t1[part[0] : part[0] + part[1], :] = total.astype(BF16)
        ex.start(("one", i))
    for h in range(4, HEADS):
        forward_out(h)
    for k in range(3):
        ex.wait(("near", k))
    for i in (1, 2):
        ex.wait(("on", i))
    for i in (1, 2, 0):
        part = PARTS[i]
        ex.wait(("one", i))
        total = own_grad[part[0] : part[0] + part[1], :] + got(r1, part, z <= 14)
        for k in range(3):
            total = total + got(near.at[k], part, y + 2**k < NY)
        if i > 0:
            total = total + got(far, part, z < 8)
        gl_ref[part[0] : part[0] + part[1], :] = total.astype(BF16)
    ex.finish()


def hand_over_kernel(*refs):
    sources, targets, held, sem = refs[:3], refs[3:6], refs[6:9], refs[9]
    into = [pltpu.make_async_copy(sources[i], held[i], sem.at[i]) for i in range(3)]
    out = [pltpu.make_async_copy(held[i], targets[i], sem.at[3 + i]) for i in range(3)]
    for copy in into:
        copy.start()
    for i in range(3):
        into[i].wait()
        out[i].start()
    for copy in out:
        copy.wait()


def hand_over(*arrays):
    hbm = pl.BlockSpec(memory_space=pltpu.HBM)
    return pl.pallas_call(
        hand_over_kernel,
        out_shape=tuple(jax.ShapeDtypeStruct(a.shape, a.dtype) for a in arrays),
        in_specs=[hbm] * 3,
        out_specs=(hbm,) * 3,
        scratch_shapes=[pltpu.VMEM(a.shape, a.dtype) for a in arrays] + [pltpu.SemaphoreType.DMA((6,))],
        compiler_params=pltpu.CompilerParams(vmem_limit_bytes=60 * 2**20),
        name="hand_over",
    )(*arrays)


def on_device(queries, latents, key_up, value_up, link_mask, out_grad):
    vmem = pl.BlockSpec(memory_space=pltpu.VMEM)
    hbm = pl.BlockSpec(memory_space=pltpu.HBM)
    block = pltpu.VMEM((WIRE, 128), BF16)
    keyed = pltpu.VMEM((SLOTS * TOK, WIDTH), BF16)
    passed = pltpu.VMEM((2, 192, 128), BF16)
    attention, grad_queries, grad_latents = pl.pallas_call(
        kernel,
        out_shape=(
            jax.ShapeDtypeStruct((TOK, WIDTH), BF16),
            jax.ShapeDtypeStruct((TOK, HEADS * (NOPE + ROPE)), BF16),
            jax.ShapeDtypeStruct((WIRE, TOK), BF16),
        ),
        in_specs=[pl.BlockSpec(memory_space=pltpu.SMEM)] + [hbm] * 5,
        out_specs=(vmem,) * 3,
        scratch_shapes=[
            pltpu.VMEM((TOK, HEADS * (NOPE + ROPE)), BF16),
            pltpu.VMEM((LATENT, WIDTH), BF16),
            pltpu.VMEM((LATENT, WIDTH), BF16),
            pltpu.VMEM((TOK, WIDTH), BF16),
            pltpu.VMEM((LEVELS, WIRE, 128), BF16),
            passed,
            pltpu.VMEM((TOK, HEADS * 256), BF16),
            keyed,
            keyed,
            pltpu.VMEM((SLOTS * TOK, 128), BF16),
            pltpu.VMEM((HEADS, TOK, 2 * TOK), F32),
            pltpu.VMEM((HEADS, TOK, 2 * TOK), F32),
            pltpu.VMEM((HEADS, TOK, 1), F32),
            pltpu.VMEM((HEADS, TOK, 1), F32),
            pltpu.VMEM((HEADS, TOK, 1), F32),
            pltpu.VMEM((HEADS, TOK, 4 * TOK), BF16),
            pltpu.VMEM((HEADS, TOK, 4 * TOK), BF16),
            keyed,
            keyed,
            pltpu.VMEM((3, WIRE, 128), BF16),
            pltpu.VMEM((LEVELS - 1, WIRE, 128), BF16),
            pltpu.VMEM((WIRE, 128), F32),
            pltpu.VMEM((192, 128), BF16),
            block, block, block, block, block, block,
            passed,
            block,
            pltpu.VMEM((3, WIRE, 128), BF16),
            pltpu.VMEM((3, WIRE, 128), BF16),
            pltpu.SemaphoreType.DMA((5,)),
            pltpu.SemaphoreType.DMA((MOVES,)),
            pltpu.SemaphoreType.DMA((MOVES,)),
        ],
        compiler_params=pltpu.CompilerParams(
            collective_id=0, has_side_effects=True, vmem_limit_bytes=60 * 2**20
        ),
        name="attend",
    )(link_mask, queries, latents.T, key_up, value_up, out_grad)
    attention, grad_queries, grad_latents = hand_over(attention, grad_queries, grad_latents)
    return attention, grad_queries, grad_latents.T


def solution(mesh):
    split = P(("dp", "ctx"), None)
    return jax.shard_map(
        on_device,
        mesh=mesh,
        in_specs=(split, split, P(), P(), split, split),
        out_specs=(split, split, split),
        check_vma=False,
    )
```

```python
import jax
import jax.numpy as jnp
from jax import lax
from jax.experimental import pallas as pl
from jax.experimental.pallas import tpu as pltpu
from jax.sharding import PartitionSpec as P

HEADS = 8
NOPE = 128
ROPE = 64
LATENT = 512
SLOTS = 4
TOK = 128
NY = 8
NZ = 16
LEVELS = 8
WIDTH = HEADS * NOPE
WIRE = LATENT + ROPE
PART_A = (384, 192)
PART_B = ((0, 192), (192, 192))
PARTS = (PART_A,) + PART_B
MESH = pl.DeviceIdType.MESH
F32 = jnp.float32
BF16 = jnp.bfloat16


class Move:
    def __init__(self, src, dst, dz, dy, valid):
        self.src, self.dst, self.dz, self.dy, self.valid = src, dst, dz, dy, valid


class Exchange:
    def __init__(self, moves, send_sem, recv_sem):
        self.moves, self.send_sem, self.recv_sem = moves, send_sem, recv_sem
        self.order = {name: i for i, name in enumerate(moves)}
        position = lax.axis_index("ctx")
        self.z = lax.div(position, NY)
        self.y = lax.rem(position, NY)

    def at(self, dz, dy):
        return lax.rem(self.z + dz + NZ, NZ), lax.rem(self.y + dy + NY, NY)

    def index(self, dz, dy):
        z, y = self.at(dz, dy)
        return z * NY + y

    def sends(self, name):
        return self.moves[name].valid(self.z, self.y)

    def receives(self, name):
        move = self.moves[name]
        return move.valid(*self.at(-move.dz, -move.dy))

    def barrier(self):
        barrier = pltpu.get_barrier_semaphore()
        groups = {}
        for name, move in self.moves.items():
            groups.setdefault((move.dz, move.dy), []).append(name)
        waits = jnp.int32(0)
        for (dz, dy), names in groups.items():
            out, into = self.sends(names[0]), self.receives(names[0])
            for name in names[1:]:
                out, into = out | self.sends(name), into | self.receives(name)
            waits = waits + out.astype(jnp.int32)

            @pl.when(into)
            def _():
                pl.semaphore_signal(
                    barrier, inc=1, device_id={"ctx": self.index(-dz, -dy)}, device_id_type=MESH
                )

        pl.semaphore_wait(barrier, waits)

    def copy(self, name):
        move, i = self.moves[name], self.order[name]
        return pltpu.make_async_remote_copy(
            src_ref=move.src,
            dst_ref=move.dst,
            send_sem=self.send_sem.at[i],
            recv_sem=self.recv_sem.at[i],
            device_id={"ctx": self.index(move.dz, move.dy)},
            device_id_type=MESH,
        )

    def start(self, name):
        @pl.when(self.sends(name))
        def _():
            self.copy(name).start()

    def wait(self, name):
        @pl.when(self.receives(name))
        def _():
            self.copy(name).wait_recv()

    def finish(self):
        for name in self.moves:

            @pl.when(self.sends(name))
            def _():
                self.copy(name).wait_send()


def rows(ref, part, lead=None):
    window = pl.ds(part[0], part[1])
    return ref.at[window] if lead is None else ref.at[lead, window]


def outward_moves(own, cand, passed):
    moves = {}
    for i, part in enumerate(PARTS):
        mine, l4, l5 = rows(own, part), rows(cand, part, 4), rows(cand, part, 5)
        l6, l7 = rows(cand, part, 6), rows(cand, part, 7)
        moves["out one", i] = Move(mine, l4, 1, 0, lambda z, y: z < 15)
        moves["out two", i] = Move(l4, l5, 1, 0, lambda z, y: (z >= 1) & (z < 15))
        moves["out four", i] = Move(l5, l6, 2, 0, lambda z, y: (z >= 2) & (z < 14))
        if i == 0:
            moves["out eight", i] = Move(l6, l7, 4, 0, lambda z, y: (z >= 4) & (z < 12))
        else:
            via = passed.at[i - 1]
            moves["out back", i] = Move(mine, via, -4, 0, lambda z, y: z < 8)
            moves["out on", i] = Move(via, l7, -4, 0, lambda z, y: (z < 4) | (z >= 12))
    for k in range(3):
        by = 2**k
        moves["out near", k] = Move(own, cand.at[k + 1], 0, by, lambda z, y, by=by: y + by < NY)
        for i, part in enumerate(PARTS):
            moves["out cross", k, i] = Move(
                rows(cand, part, 4), rows(cand, part, k + 1), 0, by,
                lambda z, y, by=by: (y + by >= NY) & (z >= 1),
            )
    return moves


def homeward_moves(pieces, r8, r4, r2, r1, t4, t2, t1, passed, far, near):
    moves = {}
    for i, part in enumerate(PARTS):
        p7 = rows(pieces, part, 6)
        if i == 0:
            moves["eight", i] = Move(p7, r8, -4, 0, lambda z, y: z >= 8)
            src = rows(t4, part)
        else:
            via, last = passed.at[i - 1], rows(far, part)
            moves["back", i] = Move(p7, via, 4, 0, lambda z, y: z >= 8)
            moves["on", i] = Move(via, last, 4, 0, lambda z, y: (z < 4) | (z >= 12))
            src = rows(pieces, part, 5)
        moves["four", i] = Move(src, rows(r4, part), -2, 0, lambda z, y: z >= 4)
        moves["two", i] = Move(rows(t2, part), rows(r2, part), -1, 0, lambda z, y: z >= 2)
        moves["one", i] = Move(rows(t1, part), rows(r1, part), -1, 0, lambda z, y: z >= 1)
    for k in range(3):
        by = 2**k
        moves["near", k] = Move(
            pieces.at[k], near.at[k], 0, -by, lambda z, y, by=by: (y >= by) | (z >= 1)
        )
    return moves


MOVES = 26 + 17
NT = (((1,), (1,)), ((), ()))
TN = (((0,), (0,)), ((), ()))


def dot(a, b, dims=(((1,), (0,)), ((), ()))):
    return lax.dot_general(a, b, dims, preferred_element_type=F32)


def kernel(
    mask_ref, q_hbm, lat_hbm, ku_hbm, vu_hbm, og_hbm, att_ref, gq_ref, gl_ref,
    q_ref, ku_ref, vu_ref, og_ref, cand, out_passed,
    qa, keys, values, rope, near_powers, near_dprobs, near_peak, near_sum, near_dot, probs, dscores, pk, pv,
    share, pieces, own_grad, r8, r4, r2, r1, t4, t2, t1, passed, far, near,
    local_sem, send_sem, recv_sem,
):
    moves = outward_moves(lat_hbm, cand, out_passed)
    moves.update(homeward_moves(pieces, r8, r4, r2, r1, t4, t2, t1, passed, far, near))
    ex = Exchange(moves, send_sem, recv_sem)
    z, y = ex.z, ex.y
    local = {
        name: pltpu.make_async_copy(src, dst, local_sem.at[i])
        for i, (name, src, dst) in enumerate(
            (
                ("own", lat_hbm, cand.at[0]),
                ("q", q_hbm, q_ref),
                ("ku", ku_hbm, ku_ref),
                ("vu", vu_hbm, vu_ref),
                ("og", og_hbm, og_ref),
            )
        )
    }
    for copy in local.values():
        copy.start()

    position = lax.axis_index("ctx")
    first = (position >= 1) & (mask_ref[0, jnp.maximum(position - 1, 0)] == 1)
    found = jnp.int32(0)
    level_of = [jnp.int32(0), jnp.int32(0)]
    slot_of = {}
    for level in range(2, LEVELS):
        source = position - 2 ** (level - 1)
        linked = (source >= 0) & (mask_ref[0, jnp.maximum(source, 0)] == 1) & (found < 2)
        for j in range(2):
            level_of[j] = jnp.where(linked & (found == j), level, level_of[j])
        slot_of[level] = jnp.where(linked, found, 2)
        found = found + linked.astype(jnp.int32)
    scale = (NOPE + ROPE) ** -0.5
    no = -jnp.inf
    t = lax.broadcasted_iota(jnp.int32, (TOK, 2 * TOK), 0)
    s = lax.broadcasted_iota(jnp.int32, (TOK, 2 * TOK), 1)
    near_allowed = jnp.where(s < TOK, t, jnp.where(first, 2 * TOK, -1)) >= s
    far_bias = jnp.where(lax.broadcasted_iota(jnp.int32, (1, 2 * TOK), 1) < found * TOK, 0.0, no)

    def rope_rows(j, block):
        padded = jnp.concatenate([block, jnp.zeros((64, TOK), BF16)], axis=0)
        rope[j * TOK : (j + 1) * TOK, :] = padded.astype(F32).T.astype(BF16)

    def project(j, blocks):
        part = slice(j * TOK, j * TOK + blocks.shape[1])
        keys[part, :] = dot(blocks, ku_ref[...], TN).astype(BF16)
        values[part, :] = dot(blocks, vu_ref[...], TN).astype(BF16)

    def near_head(h):
        cols = slice(h * 128, (h + 1) * 128)
        k_h = jnp.concatenate([keys[: 2 * TOK, cols], rope[: 2 * TOK, :]], axis=1)
        scores = dot(qa[:, h * 256 : (h + 1) * 256], k_h, NT)
        scores = jnp.where(near_allowed, scores, no)
        peak = jnp.max(scores, axis=1, keepdims=True)
        powers = jnp.exp((scores - peak) * scale)
        dprobs = dot(og_ref[:, cols], values[: 2 * TOK, cols], NT)
        near_powers[h] = powers
        near_dprobs[h] = dprobs
        near_peak[h] = peak
        near_sum[h] = jnp.sum(powers, axis=1, keepdims=True)
        near_dot[h] = jnp.sum(powers * dprobs, axis=1, keepdims=True)

    def from_y(k):
        ex.wait(("out near", k))
        for i in range(3):
            ex.wait(("out cross", k, i))

    ex.barrier()
    for i in (1, 2):
        ex.start(("out back", i))
    for i in range(3):
        ex.start(("out one", i))
    local["q"].wait()
    for h in range(HEADS):
        base = h * (NOPE + ROPE)
        qa[:, h * 256 : (h + 1) * 256] = jnp.concatenate(
            [q_ref[:, base : base + 192].astype(F32), jnp.zeros((TOK, 64), F32)], axis=1
        ).astype(BF16)
    for i in range(3):
        ex.wait(("out one", i))
        ex.start(("out two", i))
        for k in (2, 1, 0):
            ex.start(("out cross", k, i))
    for k in (0, 2, 1):
        ex.start(("out near", k))
    for name in ("own", "ku", "vu", "og"):
        local[name].wait()
    project(0, cand[0, :LATENT])
    rope_rows(0, cand[0, LATENT:])
    for i in (1, 2):
        ex.wait(("out back", i))
        ex.start(("out on", i))
    for i in range(3):
        ex.wait(("out two", i))
        ex.start(("out four", i))
    ex.wait(("out four", 0))
    ex.start(("out eight", 0))
    from_y(0)
    project(1, cand[1, :LATENT])
    rope_rows(1, cand[1, LATENT:])
    for h in range(HEADS):
        near_head(h)
    for i in (1, 2):
        ex.wait(("out four", i))
    for k in (1, 2):
        from_y(k)
    ex.wait(("out eight", 0))
    for i in (1, 2):
        ex.wait(("out on", i))

    far_rows = slice(2 * TOK, 4 * TOK)
    two, three = cand[level_of[0]], cand[level_of[1]]
    project(2, jnp.concatenate([two[:LATENT], three[:LATENT]], axis=1))
    rope_rows(2, two[LATENT:])
    rope_rows(3, three[LATENT:])
    rope_sum = jnp.zeros((2 * TOK, 128), F32)
    for h in range(HEADS):
        cols = slice(h * 128, (h + 1) * 128)
        q_h = qa[:, h * 256 : (h + 1) * 256]
        g_h = og_ref[:, cols]
        k_h = jnp.concatenate([keys[far_rows, cols], rope[far_rows, :]], axis=1)
        scores = dot(q_h, k_h, NT) + far_bias
        peak = jnp.maximum(near_peak[h], jnp.max(scores, axis=1, keepdims=True))
        powers = jnp.exp((scores - peak) * scale)
        near_factor = jnp.exp((near_peak[h] - peak) * scale)
        inverse = 1.0 / (near_factor * near_sum[h] + jnp.sum(powers, axis=1, keepdims=True))
        near_factor = near_factor * inverse
        prob = powers * inverse
        dprobs = dot(g_h, values[far_rows, cols], NT)
        delta = near_factor * near_dot[h] + jnp.sum(prob * dprobs, axis=1, keepdims=True)
        prob_bf = prob.astype(BF16)
        dscore = (prob * (dprobs - delta) * scale).astype(BF16)
        probs[h, :, 2 * TOK :] = prob_bf
        dscores[h, :, 2 * TOK :] = dscore
        near_sum[h] = near_factor
        near_dot[h] = delta
        dk = dot(dscore, q_h, TN)
        pk[far_rows, cols] = dk[:, :128].astype(BF16)
        rope_sum = rope_sum + dk[:, 128:]
        pv[far_rows, cols] = dot(prob_bf, g_h, TN).astype(BF16)
    share[2] = jnp.zeros((WIRE, 128), BF16)

    def lifted(part, tokens):
        grad = dot(ku_ref[part, :], pk[tokens, :], NT)
        return grad + dot(vu_ref[part, :], pv[tokens, :], NT)

    for i in (0, 1, 2):
        begin, end = PARTS[i][0], PARTS[i][0] + PARTS[i][1]
        grad = lifted(slice(begin, min(end, LATENT)), far_rows)
        for j in range(2):
            share[j, begin : min(end, LATENT), :] = grad[:, j * TOK : (j + 1) * TOK].astype(BF16)
            if i == 0:
                turned = rope_sum[j * TOK : (j + 1) * TOK].T
                share[j, LATENT:, :] = turned[:ROPE].astype(BF16)
        for level in (7, 6, 5, 4, 3, 2):
            pieces[level - 1, begin:end, :] = share[slot_of[level], begin:end, :]
        if i > 0:
            ex.start(("back", i))
            ex.start(("four", i))
        else:
            ex.start(("eight", 0))
    for k in (2, 1):
        ex.start(("near", k))

    def piece(level, part):
        return pieces[level - 1, part[0] : part[0] + part[1], :].astype(F32)

    def got(ref, part, valid):
        return jnp.where(valid, ref[part[0] : part[0] + part[1], :].astype(F32), 0.0)

    near_rows = slice(0, 2 * TOK)
    rope_sum = jnp.zeros((2 * TOK, 128), F32)
    for h in range(HEADS):
        cols = slice(h * 128, (h + 1) * 128)
        prob = near_powers[h] * near_sum[h]
        prob_bf = prob.astype(BF16)
        dscore = (prob * (near_dprobs[h] - near_dot[h]) * scale).astype(BF16)
        probs[h, :, : 2 * TOK] = prob_bf
        dscores[h, :, : 2 * TOK] = dscore
        dk = dot(dscore, qa[:, h * 256 : (h + 1) * 256], TN)
        pk[near_rows, cols] = dk[:, :128].astype(BF16)
        rope_sum = rope_sum + dk[:, 128:]
        pv[near_rows, cols] = dot(prob_bf, og_ref[:, cols], TN).astype(BF16)
    grad = lifted(slice(0, LATENT), near_rows)
    own_grad[:LATENT, :] = grad[:, :TOK]
    own_grad[LATENT:, :] = rope_sum[:TOK].T[:ROPE]
    pieces[0, :LATENT, :] = grad[:, TOK:].astype(BF16)
    pieces[0, LATENT:, :] = rope_sum[TOK:].T[:ROPE].astype(BF16)
    ex.start(("near", 0))

    ex.wait(("eight", 0))
    a0, a1 = PART_A[0], PART_A[0] + PART_A[1]
    t4[a0:a1, :] = (piece(6, PART_A) + jnp.where(z <= 11, r8[...].astype(F32), 0.0)).astype(BF16)
    ex.start(("four", 0))
    for i in (1, 2):
        ex.wait(("back", i))
        ex.start(("on", i))

    def forward_out(h):
        cols = slice(h * 128, (h + 1) * 128)
        base = h * (NOPE + ROPE)
        att_ref[:, cols] = dot(probs[h], values[:, cols]).astype(BF16)
        k_h = jnp.concatenate([keys[:, cols], rope[...]], axis=1)
        gq_ref[:, base : base + 192] = dot(dscores[h], k_h)[:, :192].astype(BF16)

    for i in (1, 2, 0):
        part = PARTS[i]
        ex.wait(("four", i))
        t2[part[0] : part[0] + part[1], :] = (
            piece(5, part) + got(r4, part, z <= 13)
        ).astype(BF16)
        ex.start(("two", i))
    for k in range(3):
        ex.wait(("near", k))
    for i in (1, 2, 0):
        part = PARTS[i]
        ex.wait(("two", i))
        total = piece(4, part) + got(r2, part, z <= 14)
        for k in range(3):
            total = total + got(near.at[k], part, y + 2**k >= NY)
        t1[part[0] : part[0] + part[1], :] = total.astype(BF16)
        ex.start(("one", i))
    for h in range(HEADS):
        forward_out(h)
    for i in (1, 2):
        ex.wait(("on", i))
    for i in (1, 2, 0):
        part = PARTS[i]
        ex.wait(("one", i))
        total = own_grad[part[0] : part[0] + part[1], :] + got(r1, part, z <= 14)
        for k in range(3):
            total = total + got(near.at[k], part, y + 2**k < NY)
        if i > 0:
            total = total + got(far, part, z < 8)
        gl_ref[part[0] : part[0] + part[1], :] = total.astype(BF16)
    ex.finish()


def hand_over_kernel(*refs):
    sources, targets, held, sem = refs[:3], refs[3:6], refs[6:9], refs[9]
    into = [pltpu.make_async_copy(sources[i], held[i], sem.at[i]) for i in range(3)]
    out = [pltpu.make_async_copy(held[i], targets[i], sem.at[3 + i]) for i in range(3)]
    for copy in into:
        copy.start()
    for i in range(3):
        into[i].wait()
        out[i].start()
    for copy in out:
        copy.wait()


def hand_over(*arrays):
    hbm = pl.BlockSpec(memory_space=pltpu.HBM)
    return pl.pallas_call(
        hand_over_kernel,
        out_shape=tuple(jax.ShapeDtypeStruct(a.shape, a.dtype) for a in arrays),
        in_specs=[hbm] * 3,
        out_specs=(hbm,) * 3,
        scratch_shapes=[pltpu.VMEM(a.shape, a.dtype) for a in arrays] + [pltpu.SemaphoreType.DMA((6,))],
        compiler_params=pltpu.CompilerParams(vmem_limit_bytes=60 * 2**20),
        name="hand_over",
    )(*arrays)


def on_device(queries, latents, key_up, value_up, link_mask, out_grad):
    vmem = pl.BlockSpec(memory_space=pltpu.VMEM)
    hbm = pl.BlockSpec(memory_space=pltpu.HBM)
    block = pltpu.VMEM((WIRE, 128), BF16)
    keyed = pltpu.VMEM((SLOTS * TOK, WIDTH), BF16)
    passed = pltpu.VMEM((2, 192, 128), BF16)
    attention, grad_queries, grad_latents = pl.pallas_call(
        kernel,
        out_shape=(
            jax.ShapeDtypeStruct((TOK, WIDTH), BF16),
            jax.ShapeDtypeStruct((TOK, HEADS * (NOPE + ROPE)), BF16),
            jax.ShapeDtypeStruct((WIRE, TOK), BF16),
        ),
        in_specs=[pl.BlockSpec(memory_space=pltpu.SMEM)] + [hbm] * 5,
        out_specs=(vmem,) * 3,
        scratch_shapes=[
            pltpu.VMEM((TOK, HEADS * (NOPE + ROPE)), BF16),
            pltpu.VMEM((LATENT, WIDTH), BF16),
            pltpu.VMEM((LATENT, WIDTH), BF16),
            pltpu.VMEM((TOK, WIDTH), BF16),
            pltpu.VMEM((LEVELS, WIRE, 128), BF16),
            passed,
            pltpu.VMEM((TOK, HEADS * 256), BF16),
            keyed,
            keyed,
            pltpu.VMEM((SLOTS * TOK, 128), BF16),
            pltpu.VMEM((HEADS, TOK, 2 * TOK), F32),
            pltpu.VMEM((HEADS, TOK, 2 * TOK), F32),
            pltpu.VMEM((HEADS, TOK, 1), F32),
            pltpu.VMEM((HEADS, TOK, 1), F32),
            pltpu.VMEM((HEADS, TOK, 1), F32),
            pltpu.VMEM((HEADS, TOK, 4 * TOK), BF16),
            pltpu.VMEM((HEADS, TOK, 4 * TOK), BF16),
            keyed,
            keyed,
            pltpu.VMEM((3, WIRE, 128), BF16),
            pltpu.VMEM((LEVELS - 1, WIRE, 128), BF16),
            pltpu.VMEM((WIRE, 128), F32),
            pltpu.VMEM((192, 128), BF16),
            block, block, block, block, block, block,
            passed,
            block,
            pltpu.VMEM((3, WIRE, 128), BF16),
            pltpu.SemaphoreType.DMA((5,)),
            pltpu.SemaphoreType.DMA((MOVES,)),
            pltpu.SemaphoreType.DMA((MOVES,)),
        ],
        compiler_params=pltpu.CompilerParams(
            collective_id=0, has_side_effects=True, vmem_limit_bytes=60 * 2**20
        ),
        name="attend",
    )(link_mask, queries, latents.T, key_up, value_up, out_grad)
    attention, grad_queries, grad_latents = hand_over(attention, grad_queries, grad_latents)
    return attention, grad_queries, grad_latents.T


def solution(mesh):
    split = P(("dp", "ctx"), None)
    return jax.shard_map(
        on_device,
        mesh=mesh,
        in_specs=(split, split, P(), P(), split, split),
        out_specs=(split, split, split),
        check_vma=False,
    )
```
